128 devices in a mesh: rows: 32 (over x, y, core), rep: 4 (over z).
Axes of the slice: x: 4, y: 4, z: 4, core: 2. Of those that a mesh axis runs over, the one named last changes fastest.
Arguments:
- vectors: bfloat16 [65536, 1024], P(('rows', 'rep')), may hold values from -96 to 96
- list_ids: int32 [65536], P(('rows', 'rep')), may hold values from 0 to 262143, as said below
- centroids: bfloat16 [262144, 1024], P(('rows', 'rep')), may hold values from -16 to 16
- list_place: int32 [262144], replicated, may hold values from 0 to 262143, as said below
- codes_first: int32 [65536, 128], P(('rows', 'rep')), may hold values from 0 to 255
- codes_second: int32 [65536, 128], P(('rows', 'rep')), may hold values from 0 to 255
Outputs:
- codebook_first: float32 [256, 1024], P(None, 'rows')
- codebook_second: float32 [256, 1024], P(None, 'rows')
The draws below stay inside these ranges and needn't reach their ends.
Inputs may be any that keep to these rules, and one draw needn't show every extreme that they name: list_place is a permutation of the table rows. Among the rows of one device, at most 8 have list_place[list_ids] inside one device's block of 2048 table rows, and exactly 8 for some blocks of every device.
All inputs are finite; a program needn't handle non-finite values.
Results may differ from the reference program's by a relative error of at most 0.0003.
Values may be sent and summed in bfloat16 or wider, within the bound.
A program may use at most 64 MiB of HBM per device.

```python
import math
import jax
import jax.numpy as jnp
from jax import lax

D = 1024
SUB = 8
K = 256
S = 128
ROWS_DEV = 512
CENT_DEV = 2048
ROWS = 65536
CENTS = 262144


def place_helper(key):
    devices = ROWS // ROWS_DEV
    per_owner = ROWS_DEV // devices
    quarter = devices // 4
    pattern = jnp.concatenate([jnp.full((quarter,), 2 * per_owner, jnp.int32), jnp.full((devices - 2 * quarter,), per_owner, jnp.int32), jnp.zeros((quarter,), jnp.int32)])

    def one_block(block_key):
        key_rank, key_shuffle, key_bound, key_slot = jax.random.split(block_key, 4)
        owner_rank = jax.random.permutation(key_rank, devices)
        owner_counts = pattern[owner_rank]
        owner_ids = jnp.repeat(jnp.arange(devices, dtype=jnp.int32), owner_counts, total_repeat_length=ROWS_DEV)
        owner_ids = jax.random.permutation(key_shuffle, owner_ids)
        upper_bound = jax.random.randint(key_bound, (ROWS_DEV,), 1, CENT_DEV + 1)
        random_bits = jax.random.randint(key_slot, (ROWS_DEV,), 0, 1 << 20)
        return owner_ids * CENT_DEV + random_bits % upper_bound
    places = jax.vmap(one_block)(jax.random.split(jax.random.fold_in(key, 11), devices)).reshape(-1)
    list_table = jax.random.permutation(jax.random.fold_in(key, 12), CENTS).astype(jnp.int32)
    inverse = jnp.argsort(list_table, stable=True).astype(jnp.int32)
    return (list_table, inverse[places].astype(jnp.int32))


def draw_list_place(key, part):
    return place_helper(key)[0]


def draw_list_ids(key, part):
    return place_helper(key)[1]


def code_draw(key):
    key_size, key_flag, key_code = jax.random.split(key, 3)
    shrink = jax.random.randint(key_size, (S,), 0, K // 4) * jax.random.randint(key_flag, (S,), 0, 2)
    upper_bound = K - shrink
    random_bits = jax.random.randint(key_code, (ROWS, S), 0, 1 << 20)
    return (random_bits % upper_bound[None, :]).astype(jnp.int32)


def draw_codes_first(key, part):
    return code_draw(jax.random.fold_in(key, 21))


def draw_codes_second(key, part):
    return code_draw(jax.random.fold_in(key, 22))


def spiked(array, stream_key, source, target, parts, factor):
    owner, partner = [(jnp.arange(array.shape[axis_at]) // (array.shape[axis_at] // parts)).reshape([-1 if axis == axis_at else 1 for axis in range(array.ndim)]) for axis_at in (source, target)]
    chosen = jax.random.permutation(stream_key, parts)[partner]
    strong = (owner == chosen) | (owner == (partner + parts // 2) % parts)
    return jnp.where(strong, factor * array, array)


def shard_levels(own_key, shape, pieces, least, top_value):
    def one(axis_at, parts):
        heights = jax.random.uniform(jax.random.fold_in(jax.random.fold_in(own_key, 6), axis_at), (parts,), jnp.float32, least / len(pieces), top_value / len(pieces))
        return jnp.repeat(jnp.exp(heights), shape[axis_at] // parts).reshape((-1,) + (1,) * (len(shape) - axis_at - 1))

    factor_of = one(*pieces[0])
    for cut in pieces[1:]:
        factor_of = factor_of * one(*cut)
    return factor_of


def bell_draw(rng, extent, spread, most, pieces=(), held_as=jnp.bfloat16):
    array = spread * jax.random.normal(rng, extent, jnp.float32)
    if pieces:
        array = array * shard_levels(rng, extent, pieces, -0.22, 0.18)
    return jnp.clip(array, -most, most).astype(held_as)


def noise_with(stream_key, dims, width, most, shards, heavy, kind=jnp.bfloat16):
    values = width * jax.random.normal(stream_key, dims, jnp.float32)
    if shards:
        values = values * shard_levels(stream_key, dims, shards, -0.22, 0.18)
    return jnp.clip(spiked(values, jax.random.fold_in(stream_key, 3), *heavy), -most, most).astype(kind)


def setup_inputs(seed: int = 0) -> dict:
    streams_of = jax.random.split(jax.random.key(seed), 7)
    return {
        "vectors": noise_with(streams_of[0], (ROWS, D), 4.0, 96.0, ((0, 128),), (0, 1, 128, 5.5)),
        "list_ids": draw_list_ids(jax.random.fold_in(streams_of[6], 71), 0),
        "centroids": bell_draw(streams_of[2], (CENTS, D), 4.0, 16.0, ((0, 128),)),
        "list_place": draw_list_place(jax.random.fold_in(streams_of[6], 71), 0),
        "codes_first": draw_codes_first(jax.random.fold_in(streams_of[6], 71), 0),
        "codes_second": draw_codes_second(jax.random.fold_in(streams_of[6], 71), 0),
    }


def reference(vectors, list_ids, centroids, list_place, codes_first, codes_second):
    block_rows = math.gcd(ROWS, 16384)
    turn_count = ROWS // block_rows
    offsets = jnp.arange(S, dtype=jnp.int32)[None, :] * K

    def add_block(running, block_index):
        row_start = (block_index * block_rows).astype(jnp.int32)
        row_data = lax.dynamic_slice_in_dim(vectors, row_start, block_rows, 0)
        list_block = lax.dynamic_slice_in_dim(list_ids, row_start, block_rows, 0)
        fetched_rows = jnp.take(centroids, jnp.take(list_place, list_block, axis=0), axis=0)
        residual = (row_data.astype(jnp.float32) - fetched_rows.astype(jnp.float32)).reshape(block_rows * S, SUB)
        updated = []
        for code_all, state in zip((codes_first, codes_second), running):
            code_block = lax.dynamic_slice_in_dim(code_all, row_start, block_rows, 0)
            segment = (code_block + offsets).reshape(-1)
            new_sums = state[0] + jax.ops.segment_sum(residual, segment, num_segments=S * K)
            new_counts = state[1] + jax.ops.segment_sum(jnp.ones((block_rows * S,), jnp.float32), segment, num_segments=S * K)
            updated.append((new_sums, new_counts))
        return tuple(updated), None

    zeros_sums = jnp.zeros((S * K, SUB), jnp.float32)
    zeros_counts = jnp.zeros((S * K,), jnp.float32)
    start_state = ((zeros_sums, zeros_counts), (zeros_sums, zeros_counts))
    final_state, unused = lax.scan(add_block, start_state, jnp.arange(turn_count, dtype=jnp.int32))
    codebooks = []
    for sums_part, counts_part in final_state:
        means = sums_part / jnp.maximum(counts_part, 1.0)[:, None]
        codebooks.append(jnp.transpose(means.reshape(S, K, SUB), (1, 0, 2)).reshape(K, D))
    return (codebooks[0], codebooks[1])
```

```python
import functools

import jax
import jax.numpy as jnp
from jax import lax
from jax.experimental import pallas as pl
from jax.experimental.pallas import tpu as pltpu
from jax.sharding import PartitionSpec as P

SUB = 8
K = 256
DEV = 128
CAP = 8
ROWS_DEV = 512
CENT_DEV = 2048
S = 128
D = 1024
MESH = pl.DeviceIdType.MESH
F32 = jnp.float32
BF16 = jnp.bfloat16


def iota(shape, dim):
    return lax.broadcasted_iota(jnp.int32, shape, dim)


def nt(a, b):
    return lax.dot_general(a, b, (((1,), (1,)), ((), ())), preferred_element_type=F32)


def nn(a, b):
    return jnp.dot(a, b, preferred_element_type=F32)


def one_hot(match, dtype=BF16):
    return jnp.where(match, 1.0, 0.0).astype(dtype)


def exchange_kernel(ids, place, first, second, recv, found, send, send_sem, recv_sem):
    rows_at = lax.axis_index("rows")
    rep_at = lax.axis_index("rep")
    me = rows_at * 4 + rep_at
    barrier = pltpu.get_barrier_semaphore()

    def greet(step, unused):
        other = lax.rem(me + step, DEV)
        pl.semaphore_signal(
            barrier, inc=1, device_id=(other // 4, lax.rem(other, 4)), device_id_type=MESH
        )
        return unused

    lax.fori_loop(1, DEV, greet, 0)

    lanes = iota((1, 128), 1)

    def find(block, unused):
        for step in range(8):
            row = block * 8 + step
            wanted = ids[row]
            found[pl.ds(row, 1), :] = jnp.where(
                lanes == (wanted & 127), place[pl.ds(wanted >> 7, 1), :], 0
            )
        return unused

    lax.fori_loop(0, ROWS_DEV // 8, find, 0)

    places = found[...]
    owner = (places >> 11).astype(F32).astype(BF16)
    slot_high = ((places >> 7) & 15).astype(F32).astype(BF16)
    slot_low = (places & 127).astype(F32).astype(BF16)
    owner_row = nt(jnp.ones((8, 128), BF16), owner)[0:1, :].astype(jnp.int32)
    owner_is = iota((DEV, ROWS_DEV), 0) == owner_row
    earlier = one_hot(iota((ROWS_DEV, ROWS_DEV), 0) < iota((ROWS_DEV, ROWS_DEV), 1))
    before = nn(one_hot(owner_is), earlier)
    rank = jnp.sum(jnp.where(owner_is, before, 0.0), axis=0, keepdims=True)
    position = owner_row * CAP + rank.astype(jnp.int32)
    move = one_hot(iota((DEV * CAP, ROWS_DEV), 0) == position)
    ones = jnp.ones((128, 128), BF16)
    payload = jnp.concatenate(
        [
            (first[...] + 1).astype(F32).astype(BF16),
            (second[...] + 1).astype(F32).astype(BF16),
            nn(slot_high, ones).astype(BF16),
            nn(slot_low, ones).astype(BF16),
        ],
        axis=1,
    )
    moved = nn(move, payload).astype(jnp.int32)
    codes = moved[:, 0:128] + moved[:, 128:256] * 65536
    slots = moved[:, 256:384] * 128 + moved[:, 384:512]
    send[:, 0:8, :] = codes.reshape(DEV, CAP, 128)
    send[:, 8:16, :] = slots.reshape(DEV, CAP, 128)

    pl.semaphore_wait(barrier, DEV - 1)

    def push(step, unused):
        other = lax.rem(me + step, DEV)
        pltpu.make_async_remote_copy(
            src_ref=send.at[other],
            dst_ref=recv.at[step],
            send_sem=send_sem,
            recv_sem=recv_sem,
            device_id=(other // 4, lax.rem(other, 4)),
            device_id_type=MESH,
        ).start()
        return unused

    lax.fori_loop(1, DEV, push, 0)
    recv[0] = send[me]
    rest = recv.at[pl.ds(1, DEV - 1)]
    pltpu.make_async_copy(rest, rest, recv_sem).wait()
    pltpu.make_async_copy(rest, rest, send_sem).wait()


def exchange(ids, place, first, second):
    return pl.pallas_call(
        exchange_kernel,
        out_shape=jax.ShapeDtypeStruct((DEV, 16, 128), jnp.int32),
        in_specs=[pl.BlockSpec(memory_space=pltpu.SMEM)]
        + [pl.BlockSpec(memory_space=pltpu.VMEM)] * 3,
        out_specs=pl.BlockSpec(memory_space=pltpu.VMEM),
        scratch_shapes=[
            pltpu.VMEM((ROWS_DEV, 128), jnp.int32),
            pltpu.VMEM((DEV, 16, 128), jnp.int32),
            pltpu.SemaphoreType.DMA,
            pltpu.SemaphoreType.DMA,
        ],
        compiler_params=pltpu.CompilerParams(
            collective_id=0, has_side_effects=True, vmem_limit_bytes=40 * 2**20
        ),
        name="exchange",
    )(ids, place, first, second)


ALL_ROWS = ROWS_DEV + DEV * CAP
CHUNK = 256


def sums_kernel(vectors, first, second, recv, table, out, spread, high, low):
    at = iota((512, 256), 0)
    pick = ((at >> 4) * 8 + (at & 7)) == iota((512, 256), 1)
    plus = one_hot(pick)
    minus = -plus
    eye = one_hot(iota((128, 128), 0) == iota((128, 128), 1))

    def lay_codes(codes_column, index, start):
        turned = nt(eye, codes_column.astype(F32).astype(BF16)) - 1.0
        high_part = jnp.floor(turned * 0.125)
        high[index, :, start : start + CHUNK] = high_part
        low[index, :, start : start + CHUNK] = turned - 8.0 * high_part

    for part in range(ROWS_DEV // CHUNK):
        start = part * CHUNK
        for block in range(D // 256):
            cut = vectors[start : start + CHUNK, block * 256 : (block + 1) * 256]
            spread[block * 512 : (block + 1) * 512, start : start + CHUNK] = nt(plus, cut).astype(BF16)
        lay_codes(first[start : start + CHUNK, :] + 1, 0, start)
        lay_codes(second[start : start + CHUNK, :] + 1, 1, start)

    for part in range(DEV * CAP // CHUNK):
        start = ROWS_DEV + part * CHUNK
        sources = CHUNK // CAP
        block_codes = recv[part * sources : (part + 1) * sources, 0:8, :].reshape(CHUNK, 128)
        slots = recv[part * sources : (part + 1) * sources, 8:16, :].reshape(CHUNK, 128)
        lay_codes(block_codes & 65535, 0, start)
        lay_codes(block_codes >> 16, 1, start)
        wanted = jnp.concatenate(
            [
                one_hot(slots == iota((CHUNK, 128), 1) + 128 * j)
                for j in range(CENT_DEV // 128)
            ],
            axis=1,
        )
        base = nn(wanted, table[...]).astype(BF16)
        for block in range(D // 256):
            cut = base[:, block * 256 : (block + 1) * 256]
            spread[block * 512 : (block + 1) * 512, start : start + CHUNK] = nt(minus, cut).astype(BF16)

    high_is = iota((32, CHUNK), 0).astype(F32).astype(BF16)
    low_is = (iota((64, CHUNK), 0) >> 3).astype(F32).astype(BF16)
    count_at = iota((16, CHUNK), 0)
    count_is = jnp.where(count_at < 8, count_at, -5).astype(F32).astype(BF16)
    lane_of = iota((32, 256), 1) >> 6
    count_lane_of = iota((32, 64), 1) >> 4
    one = jnp.ones((), BF16)
    zero = jnp.zeros((), BF16)

    def owner_step(owner, unused):
        counted = []
        core, spot = lax.rem(owner, 2), owner // 2
        for index in range(2):
            total = jnp.zeros((128, 256), F32)
            count = jnp.zeros((128, 64), F32)
            for part in range(ALL_ROWS // CHUNK):
                start = part * CHUNK
                left, right, mark = [], [], []
                for sub in range(4):
                    at_sub = owner * 4 + sub
                    h = high[index, pl.ds(at_sub, 1), start : start + CHUNK].astype(BF16)
                    l = low[index, pl.ds(at_sub, 1), start : start + CHUNK].astype(BF16)
                    data = spread[
                        pl.ds(pl.multiple_of(at_sub * 16, 16), 16), start : start + CHUNK
                    ]
                    left.append(jnp.where(high_is == h, one, zero))
                    four = jnp.concatenate([data] * 4, axis=0)
                    right.append(jnp.where(low_is == l, four, zero))
                    if part < ROWS_DEV // CHUNK:
                        mark.append(jnp.where(count_is == l, one, zero))
                left = jnp.concatenate(left, axis=0)
                total = total + nt(left, jnp.concatenate(right, axis=0))
                if part < ROWS_DEV // CHUNK:
                    count = count + nt(left, jnp.concatenate(mark, axis=0))
            mine = jnp.zeros((32, 256), F32)
            mine_count = jnp.zeros((32, 64), F32)
            for sub in range(4):
                mine = jnp.where(lane_of == sub, total[32 * sub : 32 * sub + 32, :], mine)
                mine_count = jnp.where(
                    count_lane_of == sub, count[32 * sub : 32 * sub + 32, :], mine_count
                )
            out[core, spot, :, 2 * index] = mine[:, 0:128].reshape(4, 8, 128)
            out[core, spot, :, 2 * index + 1] = mine[:, 128:256].reshape(4, 8, 128)
            counted.append(mine_count)
        out[core, spot, :, 4] = jnp.concatenate(counted, axis=1).reshape(4, 8, 128)
        return unused

    lax.fori_loop(0, 32, owner_step, 0)


def local_sums(vectors, first, second, recv, table):
    return pl.pallas_call(
        sums_kernel,
        out_shape=jax.ShapeDtypeStruct((2, 16, 4, 5, 8, 128), F32),
        in_specs=[pl.BlockSpec(memory_space=pltpu.VMEM)] * 5,
        out_specs=pl.BlockSpec(memory_space=pltpu.VMEM),
        scratch_shapes=[
            pltpu.VMEM((2 * D, ALL_ROWS), BF16),
            pltpu.VMEM((2, S, ALL_ROWS), F32),
            pltpu.VMEM((2, S, ALL_ROWS), F32),
        ],
        compiler_params=pltpu.CompilerParams(vmem_limit_bytes=50 * 2**20),
        name="local_sums",
    )(vectors, first, second, recv, table)


def reduce_kernel(
    parts, out, mate, half, landed, core_send, core_recv, part_send, part_recv, last_send, last_recv
):
    rows_at = lax.axis_index("rows")
    z = lax.axis_index("rep")
    core = lax.rem(rows_at, 2)
    y = lax.rem(rows_at // 2, 4)
    x = rows_at // 8
    barrier = pltpu.get_barrier_semaphore()

    def place_of(step):
        x_to = lax.rem(x + step // 16, 4)
        y_to = lax.rem(y + lax.rem(step // 4, 4), 4)
        z_to = lax.rem(z + lax.rem(step, 4), 4)
        return x_to * 4 + y_to, z_to

    mate_id = (rows_at + 1 - 2 * core, z)
    pl.semaphore_signal(barrier, inc=1, device_id=mate_id, device_id_type=MESH)

    def greet(step, unused):
        spot, z_to = place_of(step)
        pl.semaphore_signal(
            barrier, inc=1, device_id=(spot * 2 + core, z_to), device_id_type=MESH
        )
        return unused

    lax.fori_loop(1, 64, greet, 0)
    pl.semaphore_wait(barrier, 64)

    def core_copy(step):
        spot, unused = place_of(step * 4)
        return pltpu.make_async_remote_copy(
            src_ref=parts.at[1 - core, spot],
            dst_ref=mate.at[step],
            send_sem=core_send.at[step],
            recv_sem=core_recv.at[step],
            device_id=mate_id,
            device_id_type=MESH,
        )

    def start_core(step, unused):
        core_copy(lax.rem(step, 16)).start()
        return unused

    lax.fori_loop(1, 17, start_core, 0)

    def part_copy(step):
        spot, z_to = place_of(step)
        return pltpu.make_async_remote_copy(
            src_ref=half.at[step // 4, z_to],
            dst_ref=landed.at[step],
            send_sem=part_send,
            recv_sem=part_recv,
            device_id=(spot * 2 + core, z_to),
            device_id_type=MESH,
        )

    def send_parts(turn, unused):
        step = lax.rem(turn, 16)
        core_copy(step).wait_recv()
        spot, unused_z = place_of(step * 4)
        half[step] = parts[core, spot] + mate[step]

        @pl.when(step != 0)
        def _():
            part_copy(step * 4).start()

        for z_step in range(1, 4):
            part_copy(step * 4 + z_step).start()
        return unused

    lax.fori_loop(1, 17, send_parts, 0)

    rest = landed.at[pl.ds(1, 63)]
    pltpu.make_async_copy(rest, rest, part_recv).wait()

    def add(step, total):
        return total + landed[step]

    out[z] = lax.fori_loop(1, 64, add, half[0, z])

    for z_step in range(1, 4):
        pltpu.make_async_remote_copy(
            src_ref=out.at[z],
            dst_ref=out.at[z],
            send_sem=last_send,
            recv_sem=last_recv,
            device_id=(rows_at, lax.rem(z + z_step, 4)),
            device_id_type=MESH,
        ).start()
    three = landed.at[pl.ds(0, 3)]
    pltpu.make_async_copy(three, three, last_recv).wait()
    pltpu.make_async_copy(three, three, last_send).wait()
    pltpu.make_async_copy(rest, rest, part_send).wait()

    def end_core(step, unused):
        core_copy(step).wait_send()
        return unused

    lax.fori_loop(0, 16, end_core, 0)


def reduce_parts(parts):
    return pl.pallas_call(
        reduce_kernel,
        out_shape=jax.ShapeDtypeStruct((4, 5, 8, 128), F32),
        in_specs=[pl.BlockSpec(memory_space=pltpu.VMEM)],
        out_specs=pl.BlockSpec(memory_space=pltpu.VMEM),
        scratch_shapes=[
            pltpu.VMEM((16, 4, 5, 8, 128), F32),
            pltpu.VMEM((16, 4, 5, 8, 128), F32),
            pltpu.VMEM((64, 5, 8, 128), F32),
            pltpu.SemaphoreType.DMA((16,)),
            pltpu.SemaphoreType.DMA((16,)),
            pltpu.SemaphoreType.DMA,
            pltpu.SemaphoreType.DMA,
            pltpu.SemaphoreType.DMA,
            pltpu.SemaphoreType.DMA,
        ],
        compiler_params=pltpu.CompilerParams(
            collective_id=1, has_side_effects=True, vmem_limit_bytes=40 * 2**20
        ),
        name="reduce_parts",
    )(parts)


def means_kernel(total, out_first, out_second):
    count = jnp.maximum(total[:, 4].reshape(32, 128), 1.0)
    for index, out in ((0, out_first), (1, out_second)):
        sums = jnp.concatenate(
            [total[:, 2 * index].reshape(32, 128), total[:, 2 * index + 1].reshape(32, 128)], axis=1
        )
        from_lane = iota((128, 256), 0)
        lane = iota((128, 256), 1)
        fan = one_hot(from_lane == index * 64 + (lane >> 6) * 16 + ((lane >> 3) & 7), F32)
        fanned = jnp.dot(count, fan, preferred_element_type=F32, precision=lax.Precision.HIGHEST)
        means = sums / fanned
        wide = iota((256, 32), 0)
        column = iota((256, 32), 1)
        for low in range(8):
            choose = one_hot(wide == (column >> 3) * 64 + low * 8 + (column & 7), F32)
            out[pl.ds(low, 32, stride=8), :] = jnp.dot(
                means, choose, preferred_element_type=F32, precision=lax.Precision.HIGHEST
            )


def means_of(total):
    return pl.pallas_call(
        means_kernel,
        out_shape=[jax.ShapeDtypeStruct((K, 32), F32)] * 2,
        in_specs=[pl.BlockSpec(memory_space=pltpu.VMEM)],
        out_specs=[pl.BlockSpec(memory_space=pltpu.VMEM)] * 2,
        name="means",
    )(total)


def on_device(vectors, list_ids, centroids, list_place, codes_first, codes_second):
    place = list_place.reshape(2048, 128)
    recv = exchange(list_ids, place, codes_first, codes_second)
    parts = local_sums(vectors, codes_first, codes_second, recv, centroids)
    first, second = means_of(reduce_parts(parts))
    return (first, second)


def solution(mesh):
    return jax.shard_map(
        on_device,
        mesh=mesh,
        in_specs=(
            P(("rows", "rep"), None),
            P(("rows", "rep")),
            P(("rows", "rep"), None),
            P(),
            P(("rows", "rep"), None),
            P(("rows", "rep"), None),
        ),
        out_specs=(P(None, "rows"), P(None, "rows")),
        check_vma=False,
    )
```

```python
import jax
import jax.numpy as jnp
from jax import lax
from jax.experimental import pallas as pl
from jax.experimental.pallas import tpu as pltpu
from jax.sharding import PartitionSpec as P

K = 256
D = 1024
S = 128
DEV = 128
CAP = 8
ROWS_DEV = 512
CENT_DEV = 2048
ASKED = DEV * CAP
CHUNK = 256
LAG = 3
MESH = pl.DeviceIdType.MESH
F32 = jnp.float32
BF16 = jnp.bfloat16
I32 = jnp.int32


def iota(shape, dim):
    return lax.broadcasted_iota(I32, shape, dim)


def nt(a, b):
    return lax.dot_general(a, b, (((1,), (1,)), ((), ())), preferred_element_type=F32)


def nn(a, b):
    return jnp.dot(a, b, preferred_element_type=F32)


def one_hot(match):
    return jnp.where(match, 1.0, 0.0).astype(BF16)


def narrow(whole):
    return whole.astype(F32).astype(BF16)


def kernel(
    ids,
    place_hbm,
    first_hbm,
    second_hbm,
    vectors_hbm,
    table_hbm,
    out_first,
    out_second,
    place,
    first,
    second,
    vectors,
    table,
    found,
    send,
    recv,
    spread_own,
    high_own,
    low_own,
    wanted,
    spread_asked,
    high_asked,
    low_asked,
    parts,
    mate,
    half,
    landed,
    means,
    load_sem,
    send_sem,
    recv_sem,
    core_send,
    core_recv,
    part_send,
    part_recv,
    last_send,
    last_recv,
):
    rows_at = lax.axis_index("rows")
    z = lax.axis_index("rep")
    me = rows_at * 4 + z
    core = lax.rem(rows_at, 2)
    y = lax.rem(rows_at // 2, 4)
    x = rows_at // 8
    barrier = pltpu.get_barrier_semaphore()

    loads = []
    for at, (source, target) in enumerate(
        (
            (place_hbm, place),
            (first_hbm, first),
            (second_hbm, second),
            (vectors_hbm, vectors),
            (table_hbm, table),
        )
    ):
        load = pltpu.make_async_copy(source, target, load_sem.at[at])
        load.start()
        loads.append(load)

    def greet(step, unused):
        other = lax.rem(me + step, DEV)
        pl.semaphore_signal(
            barrier, inc=1, device_id=(other // 4, lax.rem(other, 4)), device_id_type=MESH
        )
        return unused

    lax.fori_loop(1, DEV, greet, 0)

    loads[0].wait()
    lanes = iota((1, 128), 1)

    def find(block, unused):
        for step in range(8):
            row = block * 8 + step
            wish = ids[row]
            found[pl.ds(row, 1), :] = jnp.where(
                lanes == (wish & 127), place[pl.ds(wish >> 7, 1), :], 0
            )
        return unused

    lax.fori_loop(0, ROWS_DEV // 8, find, 0)

    places = found[...]
    ones8 = jnp.ones((8, 128), BF16)
    owner_row = nt(ones8, narrow(places >> 11))[0:1, :].astype(I32)
    slot_high = nt(ones8, narrow((places >> 7) & 15))[0:1, :]
    slot_low = nt(ones8, narrow(places & 127))[0:1, :]
    owner_is = iota((DEV, ROWS_DEV), 0) == owner_row
    owner_hot = one_hot(owner_is)
    earlier = one_hot(iota((ROWS_DEV, ROWS_DEV), 0) < iota((ROWS_DEV, ROWS_DEV), 1))
    before = nn(owner_hot, earlier)
    rank = jnp.sum(jnp.where(owner_is, before, 0.0), axis=0, keepdims=True).astype(I32)
    rank_is = iota((DEV, ROWS_DEV), 0) == rank
    slots_high = nt(owner_hot, jnp.where(rank_is, slot_high, 0.0).astype(BF16))
    slots_low = nt(owner_hot, jnp.where(rank_is, slot_low, 0.0).astype(BF16))
    slots = (slots_high * 128.0 + slots_low).astype(I32)
    position = owner_row * CAP + rank
    loads[1].wait()
    loads[2].wait()
    payload = jnp.concatenate([narrow(first[...] + 1), narrow(second[...] + 1)], axis=1)
    for block in range(4):
        move = one_hot(iota((256, ROWS_DEV), 0) + 256 * block == position)
        moved = nn(move, payload).astype(I32)
        codes = moved[:, 0:128] + moved[:, 128:256] * 65536
        send[32 * block : 32 * block + 32, 0:8, :] = codes.reshape(32, CAP, 128)
    send[:, 8:9, :] = slots.reshape(DEV, 1, 128)

    pl.semaphore_wait(barrier, DEV - 1)

    def push(step, unused):
        other = lax.rem(me + step, DEV)
        pltpu.make_async_remote_copy(
            src_ref=send.at[other],
            dst_ref=recv.at[step],
            send_sem=send_sem,
            recv_sem=recv_sem,
            device_id=(other // 4, lax.rem(other, 4)),
            device_id_type=MESH,
        ).start()
        return unused

    lax.fori_loop(1, DEV, push, 0)
    recv[0] = send[me]

    def lay_codes(column, high, low, index, start):
        turned = nt(eye128, narrow(column)) - 1.0
        low_part = jnp.floor(turned * (1.0 / 32.0))
        high[index, :, start : start + CHUNK] = turned - 32.0 * low_part
        low[index, :, start : start + CHUNK] = low_part

    eye128 = one_hot(iota((128, 128), 0) == iota((128, 128), 1))
    eye256 = one_hot(iota((256, 256), 0) == iota((256, 256), 1))

    high_is = narrow(iota((16, CHUNK), 0))
    count_is = narrow(iota((16, CHUNK), 0) & 7)
    wide_lane = iota((32, 256), 1)
    lane_sub = (wide_lane >> 7) * 2 + ((wide_lane >> 3) & 1)
    count_lane_sub = iota((32, 32), 1) >> 3
    one = jnp.ones((), BF16)
    zero = jnp.zeros((), BF16)

    def tally(spread, row, high, low, owner, chunks, index, counting):
        total = count = None
        for chunk in range(chunks):
            start = chunk * CHUNK
            left, right, mark = [], [], []
            for pair in range(2):
                data = spread[
                    pl.ds(pl.multiple_of(row + 16 * pair, 16), 16), start : start + CHUNK
                ]
                lows = []
                for sub in range(2):
                    at = owner * 4 + pair * 2 + sub
                    h = jnp.broadcast_to(high[index, pl.ds(at, 1), start : start + CHUNK], (8, CHUNK))
                    h = jnp.concatenate([h, h], axis=0).astype(BF16)
                    left.append(jnp.where(h == high_is, one, zero))
                    left.append(jnp.where(h == high_is + 16.0, one, zero))
                    lows.append(
                        jnp.broadcast_to(low[index, pl.ds(at, 1), start : start + CHUNK], (8, CHUNK))
                    )
                l = jnp.concatenate(lows, axis=0).astype(BF16)
                for value in range(8):
                    right.append(jnp.where(l == jnp.full((), value, BF16), data, zero))
                if counting:
                    mark.append(jnp.where(l == count_is, one, zero))
            left = jnp.concatenate(left, axis=0)
            product = nt(left, jnp.concatenate(right, axis=0))
            total = product if total is None else total + product
            if counting:
                product = nt(left, jnp.concatenate(mark, axis=0))
                count = product if count is None else count + product
        mine = total[0:32]
        mine_count = count[0:32] if counting else None
        for sub in range(1, 4):
            cut = slice(32 * sub, 32 * sub + 32)
            mine = jnp.where(lane_sub == sub, total[cut], mine)
            if counting:
                mine_count = jnp.where(count_lane_sub == sub, count[cut], mine_count)
        return mine, mine_count

    def spot_of(turn):
        x_to = lax.rem(x + turn // 4 + 1, 4)
        y_to = lax.rem(y + lax.rem(turn, 4) + 1, 4)
        return x_to * 4 + y_to

    loads[3].wait()
    for chunk in range(ROWS_DEV // CHUNK):
        start = chunk * CHUNK
        for block in range(D // 256):
            cut = vectors[start : start + CHUNK, block * 256 : (block + 1) * 256]
            spread_own[block * 256 : (block + 1) * 256, start : start + CHUNK] = nt(
                eye256, cut
            ).astype(BF16)
        lay_codes(first[start : start + CHUNK, :] + 1, high_own, low_own, 0, start)
        lay_codes(second[start : start + CHUNK, :] + 1, high_own, low_own, 1, start)

    def own_step(step, unused):
        turn, side = step // 2, lax.rem(step, 2)
        owner = spot_of(turn) * 2 + side
        counted = []
        for index in range(2):
            mine, count = tally(
                spread_own, owner * 32, high_own, low_own, owner, ROWS_DEV // CHUNK, index, True
            )
            parts[side, turn, :, 2 * index] = mine[:, 0:128].reshape(4, 8, 128)
            parts[side, turn, :, 2 * index + 1] = mine[:, 128:256].reshape(4, 8, 128)
            counted.append(count)
        counted.append(jnp.zeros((32, 64), F32))
        parts[side, turn, :, 4] = jnp.concatenate(counted, axis=1).reshape(4, 8, 128)
        return unused

    lax.fori_loop(0, 32, own_step, 0)

    rest = recv.at[pl.ds(1, DEV - 1)]
    pltpu.make_async_copy(rest, rest, recv_sem).wait()
    loads[4].wait()
    ones128 = jnp.ones((128, 128), BF16)
    slots_in = recv[:, 8:9, :].reshape(DEV, 128)
    slots_high = narrow(slots_in >> 7)
    slots_low = narrow(slots_in & 127)
    for chunk in range(ASKED // CHUNK):
        start = chunk * CHUNK
        codes = recv[32 * chunk : 32 * chunk + 32, 0:8, :].reshape(CHUNK, 128)
        lay_codes(codes & 65535, high_asked, low_asked, 0, start)
        lay_codes(codes >> 16, high_asked, low_asked, 1, start)
        row_at = iota((CHUNK, 128), 0)
        lane = iota((CHUNK, 128), 1)
        fan = one_hot((row_at >> 3) + 32 * chunk == lane)
        keep = (row_at & 7) == lane
        slot_high = nn(jnp.where(keep, nn(fan, slots_high), 0.0).astype(BF16), ones128).astype(BF16)
        slot_low = nn(jnp.where(keep, nn(fan, slots_low), 0.0).astype(BF16), ones128).astype(BF16)
        low_hot = jnp.where(slot_low == narrow(lane), one, zero)
        for block in range(CENT_DEV // 128):
            wanted[start : start + CHUNK, block * 128 : (block + 1) * 128] = jnp.where(
                slot_high == jnp.full((), block, BF16), low_hot, zero
            )

    mate_id = (rows_at + 1 - 2 * core, z)

    def core_copy(turn):
        return pltpu.make_async_remote_copy(
            src_ref=parts.at[1 - core, turn],
            dst_ref=mate.at[turn],
            send_sem=core_send.at[turn],
            recv_sem=core_recv.at[turn],
            device_id=mate_id,
            device_id_type=MESH,
        )

    def part_copy(turn, z_step):
        z_to = lax.rem(z + z_step, 4)
        return pltpu.make_async_remote_copy(
            src_ref=half.at[turn, z_to],
            dst_ref=landed.at[turn * 4 + 3 - z_step],
            send_sem=part_send,
            recv_sem=part_recv,
            device_id=(spot_of(turn) * 2 + core, z_to),
            device_id_type=MESH,
        )

    def pass_on(turn):
        core_copy(turn).wait_recv()
        half[turn] = parts[core, turn] + mate[turn]
        for z_step in range(1, 4):
            part_copy(turn, z_step).start()

        @pl.when(turn != 15)
        def _():
            part_copy(turn, 0).start()

    def block_step(block, unused):
        x_to = lax.rem(x + block + 1, 4)
        columns = pl.ds(pl.multiple_of(x_to * 256, 256), 256)
        base = nn(wanted[...], table[:, columns]).astype(BF16)
        for chunk in range(ASKED // CHUNK):
            start = chunk * CHUNK
            spread_asked[:, start : start + CHUNK] = nt(-eye256, base[start : start + CHUNK]).astype(
                BF16
            )

        def spot_step(spot, unused_too):
            turn = block * 4 + spot
            y_to = lax.rem(y + spot + 1, 4)

            def side_step(side, unused_three):
                owner = spot_of(turn) * 2 + side
                for index in range(2):
                    mine, unused_count = tally(
                        spread_asked,
                        (y_to * 2 + side) * 32,
                        high_asked,
                        low_asked,
                        owner,
                        ASKED // CHUNK,
                        index,
                        False,
                    )
                    parts[side, turn, :, 2 * index] += mine[:, 0:128].reshape(4, 8, 128)
                    parts[side, turn, :, 2 * index + 1] += mine[:, 128:256].reshape(4, 8, 128)
                return unused_three

            lax.fori_loop(0, 2, side_step, 0)
            core_copy(turn).start()

            @pl.when(turn >= LAG)
            def _():
                pass_on(turn - LAG)

            return unused_too

        lax.fori_loop(0, 4, spot_step, 0)
        return unused

    lax.fori_loop(0, 4, block_step, 0)
    for turn in range(16 - LAG, 16):
        pass_on(jnp.int32(turn))

    others = landed.at[pl.ds(0, 63)]
    pltpu.make_async_copy(others, others, part_recv).wait()

    def add(step, total):
        return total + landed[step]

    total = lax.fori_loop(0, 63, add, half[15, z])

    count = jnp.maximum(total[4], 1.0)
    count_high = jnp.floor(count * (1.0 / 256.0))
    count_low = (count - 256.0 * count_high).astype(BF16)
    count_high = count_high.astype(BF16)
    from_lane = iota((128, 256), 0)
    lane = iota((128, 256), 1)
    sub_lane = ((lane >> 7) * 2 + ((lane >> 3) & 1)) * 8 + ((lane >> 4) & 7)
    for index in range(2):
        fan = one_hot(from_lane == index * 32 + sub_lane)
        fanned = 256.0 * nn(count_high, fan) + nn(count_low, fan)
        means[z, 2 * index] = total[2 * index] / fanned[:, 0:128]
        means[z, 2 * index + 1] = total[2 * index + 1] / fanned[:, 128:256]

    for z_step in range(1, 4):
        pltpu.make_async_remote_copy(
            src_ref=means.at[z],
            dst_ref=means.at[z],
            send_sem=last_send,
            recv_sem=last_recv,
            device_id=(rows_at, lax.rem(z + z_step, 4)),
            device_id_type=MESH,
        ).start()
    three = means.at[pl.ds(0, 3)]
    pltpu.make_async_copy(three, three, last_recv).wait()
    for index, out in ((0, out_first), (1, out_second)):
        both = jnp.concatenate(
            [means[:, 2 * index].reshape(32, 128), means[:, 2 * index + 1].reshape(32, 128)], axis=1
        ).T
        out[...] = jnp.concatenate(
            [
                jnp.concatenate([both[16 * v : 16 * v + 16], both[128 + 16 * v : 144 + 16 * v]], axis=0)
                for v in range(8)
            ],
            axis=1,
        )

    pltpu.make_async_copy(three, three, last_send).wait()
    pltpu.make_async_copy(others, others, part_send).wait()
    pltpu.make_async_copy(rest, rest, send_sem).wait()

    def end_core(turn, unused):
        core_copy(turn).wait_send()
        return unused

    lax.fori_loop(0, 16, end_core, 0)


def on_device(vectors, list_ids, centroids, list_place, codes_first, codes_second):
    place = list_place.reshape(2048, 128)
    vmem, dma = pltpu.VMEM, pltpu.SemaphoreType.DMA
    first, second = pl.pallas_call(
        kernel,
        out_shape=[jax.ShapeDtypeStruct((32, K), F32)] * 2,
        in_specs=[pl.BlockSpec(memory_space=pltpu.SMEM)]
        + [pl.BlockSpec(memory_space=pl.ANY)] * 5,
        out_specs=[pl.BlockSpec(memory_space=pltpu.VMEM)] * 2,
        scratch_shapes=[
            vmem((2048, 128), I32),
            vmem((ROWS_DEV, S), I32),
            vmem((ROWS_DEV, S), I32),
            vmem((ROWS_DEV, D), BF16),
            vmem((CENT_DEV, D), BF16),
            vmem((ROWS_DEV, 128), I32),
            vmem((DEV, 9, 128), I32),
            vmem((DEV, 9, 128), I32),
            vmem((D, ROWS_DEV), BF16),
            vmem((2, S, ROWS_DEV), F32),
            vmem((2, S, ROWS_DEV), F32),
            vmem((ASKED, CENT_DEV), BF16),
            vmem((256, ASKED), BF16),
            vmem((2, S, ASKED), F32),
            vmem((2, S, ASKED), F32),
            vmem((2, 16, 4, 5, 8, 128), F32),
            vmem((16, 4, 5, 8, 128), F32),
            vmem((16, 4, 5, 8, 128), F32),
            vmem((63, 5, 8, 128), F32),
            vmem((4, 4, 8, 128), F32),
            dma((5,)),
            dma,
            dma,
            dma((16,)),
            dma((16,)),
            dma,
            dma,
            dma,
            dma,
        ],
        compiler_params=pltpu.CompilerParams(
            collective_id=0, has_side_effects=True, vmem_limit_bytes=60 * 2**20
        ),
        name="codebooks",
    )(list_ids, place, codes_first, codes_second, vectors, centroids)
    return (first.T, second.T)


def solution(mesh):
    return jax.shard_map(
        on_device,
        mesh=mesh,
        in_specs=(
            P(("rows", "rep"), None),
            P(("rows", "rep")),
            P(("rows", "rep"), None),
            P(),
            P(("rows", "rep"), None),
            P(("rows", "rep"), None),
        ),
        out_specs=(P(None, "rows"), P(None, "rows")),
        check_vma=False,
    )
```

```python
import jax
import jax.numpy as jnp
from jax import lax
from jax.experimental import pallas as pl
from jax.experimental.pallas import tpu as pltpu
from jax.sharding import PartitionSpec as P

K = 256
D = 1024
S = 128
DEV = 128
CAP = 8
ROWS_DEV = 512
CENT_DEV = 2048
ASKED = DEV * CAP
CHUNK = 256
LAG = 1
MESH = pl.DeviceIdType.MESH
F32 = jnp.float32
BF16 = jnp.bfloat16
I32 = jnp.int32


def iota(shape, dim):
    return lax.broadcasted_iota(I32, shape, dim)


def nt(a, b):
    return lax.dot_general(a, b, (((1,), (1,)), ((), ())), preferred_element_type=F32)


def nn(a, b):
    return jnp.dot(a, b, preferred_element_type=F32)


def one_hot(match):
    return jnp.where(match, 1.0, 0.0).astype(BF16)


def narrow(whole):
    return whole.astype(F32).astype(BF16)


def kernel(
    ids,
    place_hbm,
    first_hbm,
    second_hbm,
    vectors_hbm,
    table_hbm,
    out_first,
    out_second,
    place,
    first,
    second,
    vectors,
    table,
    found,
    send,
    recv,
    spread_own,
    high_own,
    low_own,
    inner_own,
    outer_own,
    wanted,
    spread_asked,
    high_asked,
    low_asked,
    parts,
    mate,
    half,
    landed,
    counts,
    count_mate,
    count_half,
    count_landed,
    means,
    load_sem,
    send_sem,
    recv_sem,
    core_send,
    core_recv,
    part_send,
    part_recv,
    swap_send,
    swap_recv,
    count_send,
    count_recv,
    last_send,
    last_recv,
):
    rows_at = lax.axis_index("rows")
    z = lax.axis_index("rep")
    me = rows_at * 4 + z
    core = lax.rem(rows_at, 2)
    y = lax.rem(rows_at // 2, 4)
    x = rows_at // 8
    barrier = pltpu.get_barrier_semaphore()

    loads = []
    for at, (source, target) in enumerate(
        (
            (place_hbm, place),
            (first_hbm, first),
            (second_hbm, second),
            (vectors_hbm, vectors),
            (table_hbm, table),
        )
    ):
        load = pltpu.make_async_copy(source, target, load_sem.at[at])
        load.start()
        loads.append(load)

    def greet(step, unused):
        other = lax.rem(me + step, DEV)
        pl.semaphore_signal(
            barrier, inc=1, device_id=(other // 4, lax.rem(other, 4)), device_id_type=MESH
        )
        return unused

    lax.fori_loop(1, DEV, greet, 0)

    loads[0].wait()
    lanes = iota((1, 128), 1)

    def find(block, unused):
        for step in range(8):
            row = block * 8 + step
            wish = ids[row]
            found[pl.ds(row, 1), :] = jnp.where(
                lanes == (wish & 127), place[pl.ds(wish >> 7, 1), :], 0
            )
        return unused

    lax.fori_loop(0, ROWS_DEV // 8, find, 0)

    places = found[...]
    ones8 = jnp.ones((8, 128), BF16)
    owner_row = nt(ones8, narrow(places >> 11))[0:1, :].astype(I32)
    slot_high = nt(ones8, narrow((places >> 7) & 15))[0:1, :]
    slot_low = nt(ones8, narrow(places & 127))[0:1, :]
    owner_is = iota((DEV, ROWS_DEV), 0) == owner_row
    owner_hot = one_hot(owner_is)
    earlier = one_hot(iota((ROWS_DEV, ROWS_DEV), 0) < iota((ROWS_DEV, ROWS_DEV), 1))
    before = nn(owner_hot, earlier)
    rank = jnp.sum(jnp.where(owner_is, before, 0.0), axis=0, keepdims=True).astype(I32)
    rank_is = iota((DEV, ROWS_DEV), 0) == rank
    slots_high = nt(owner_hot, jnp.where(rank_is, slot_high, 0.0).astype(BF16))
    slots_low = nt(owner_hot, jnp.where(rank_is, slot_low, 0.0).astype(BF16))
    slots = (slots_high * 128.0 + slots_low).astype(I32)
    position = owner_row * CAP + rank
    loads[1].wait()
    loads[2].wait()
    payload = jnp.concatenate([narrow(first[...] + 1), narrow(second[...] + 1)], axis=1)
    for block in range(4):
        move = one_hot(iota((256, ROWS_DEV), 0) + 256 * block == position)
        moved = nn(move, payload).astype(I32)
        codes = moved[:, 0:128] + moved[:, 128:256] * 65536
        send[32 * block : 32 * block + 32, 0:8, :] = codes.reshape(32, CAP, 128)
    send[:, 8:9, :] = slots.reshape(DEV, 1, 128)

    pl.semaphore_wait(barrier, DEV - 1)

    def push(step, unused):
        other = lax.rem(me + step, DEV)
        pltpu.make_async_remote_copy(
            src_ref=send.at[other],
            dst_ref=recv.at[step],
            send_sem=send_sem,
            recv_sem=recv_sem.at[step >> 5],
            device_id=(other >> 2, other & 3),
            device_id_type=MESH,
        ).start()
        return unused

    lax.fori_loop(1, DEV, push, 0)
    recv[0] = send[me]

    def lay_codes(column, high, low, index, start):
        turned = nt(eye128, narrow(column)) - 1.0
        low_part = jnp.floor(turned * (1.0 / 32.0))
        high_part = turned - 32.0 * low_part
        high[index, :, start : start + CHUNK] = high_part
        low[index, :, start : start + CHUNK] = low_part
        return high_part, low_part

    def lay_own(column, index, start):
        high_part, low_part = lay_codes(column, high_own, low_own, index, start)
        odd = jnp.where(high_part >= 16.0, 1.0, 0.0)
        inner_own[index, :, start : start + CHUNK] = high_part - 16.0 * odd
        outer_own[index, :, start : start + CHUNK] = low_part + 8.0 * odd

    eye128 = one_hot(iota((128, 128), 0) == iota((128, 128), 1))
    eye256 = one_hot(iota((256, 256), 0) == iota((256, 256), 1))

    high_is = narrow(iota((16, CHUNK), 0))
    wide_lane = iota((32, 256), 1)
    lane_sub = (wide_lane >> 7) * 2 + ((wide_lane >> 3) & 1)
    one = jnp.ones((), BF16)
    zero = jnp.zeros((), BF16)

    def tally(spread, row, high, low, owner, chunks, index):
        total = None
        for chunk in chunks:
            start = chunk * CHUNK
            left, right = [], []
            for pair in range(2):
                data = spread[
                    pl.ds(pl.multiple_of(row + 16 * pair, 16), 16), start : start + CHUNK
                ]
                lows = []
                for sub in range(2):
                    at = owner * 4 + pair * 2 + sub
                    h = jnp.broadcast_to(high[index, pl.ds(at, 1), start : start + CHUNK], (8, CHUNK))
                    h = jnp.concatenate([h, h], axis=0).astype(BF16)
                    left.append(jnp.where(h == high_is, one, zero))
                    left.append(jnp.where(h == high_is + 16.0, one, zero))
                    lows.append(
                        jnp.broadcast_to(low[index, pl.ds(at, 1), start : start + CHUNK], (8, CHUNK))
                    )
                l = jnp.concatenate(lows, axis=0).astype(BF16)
                for value in range(8):
                    right.append(jnp.where(l == jnp.full((), value, BF16), data, zero))
            product = nt(jnp.concatenate(left, axis=0), jnp.concatenate(right, axis=0))
            total = product if total is None else total + product
        mine = total[0:32]
        for sub in range(1, 4):
            mine = jnp.where(lane_sub == sub, total[32 * sub : 32 * sub + 32], mine)
        return mine

    def spot_of(turn):
        x_to = lax.rem(x + turn // 4 + 1, 4)
        y_to = lax.rem(y + lax.rem(turn, 4) + 1, 4)
        return x_to * 4 + y_to

    loads[3].wait()
    for chunk in range(ROWS_DEV // CHUNK):
        start = chunk * CHUNK
        for block in range(D // 256):
            cut = vectors[start : start + CHUNK, block * 256 : (block + 1) * 256]
            spread_own[block * 256 : (block + 1) * 256, start : start + CHUNK] = nt(
                eye256, cut
            ).astype(BF16)
        lay_own(first[start : start + CHUNK, :] + 1, 0, start)
        lay_own(second[start : start + CHUNK, :] + 1, 1, start)

    def own_step(turn, unused):
        for side in range(2):
            owner = spot_of(turn) * 2 + side
            for index in range(2):
                mine = tally(
                    spread_own, owner * 32, high_own, low_own, owner, range(ROWS_DEV // CHUNK), index
                )
                parts[side, turn, :, 2 * index] = mine[:, 0:128].reshape(4, 8, 128)
                parts[side, turn, :, 2 * index + 1] = mine[:, 128:256].reshape(4, 8, 128)
        return unused


    sixteen = narrow(iota((16, CHUNK), 0))
    count_lane = iota((16, 256), 1) >> 4

    def count_step(turn, unused):
        total = None
        for chunk in range(ROWS_DEV // CHUNK):
            start = chunk * CHUNK
            left, right = [], []
            for side in range(2):
                for index in range(2):
                    for sub in range(4):
                        at = pl.ds((spot_of(turn) * 2 + side) * 4 + sub, 1)
                        for source, target in ((inner_own, left), (outer_own, right)):
                            code = jnp.broadcast_to(
                                source[index, at, start : start + CHUNK], (8, CHUNK)
                            )
                            code = jnp.concatenate([code, code], axis=0).astype(BF16)
                            target.append(jnp.where(code == sixteen, one, zero))
            product = nt(jnp.concatenate(left, axis=0), jnp.concatenate(right, axis=0))
            total = product if total is None else total + product
        mine = total[0:16]
        for at in range(1, 16):
            mine = jnp.where(count_lane == at, total[16 * at : 16 * at + 16], mine)
        for side in range(2):
            counts[side, turn] = mine[:, 128 * side : 128 * side + 128].reshape(2, 8, 128)
        return unused

    lax.fori_loop(0, 16, count_step, 0)

    mate_id = (rows_at + 1 - 2 * core, z)
    count_swap = pltpu.make_async_remote_copy(
        src_ref=counts.at[1 - core],
        dst_ref=count_mate,
        send_sem=swap_send,
        recv_sem=swap_recv,
        device_id=mate_id,
        device_id_type=MESH,
    )
    count_swap.start()
    lax.fori_loop(0, 16, own_step, 0)

    def count_copy(turn, z_step):
        z_to = lax.rem(z + z_step, 4)
        return pltpu.make_async_remote_copy(
            src_ref=count_half.at[turn, lax.rem(z_to, 2)],
            dst_ref=count_landed.at[turn * 4 + 3 - z_step],
            send_sem=count_send,
            recv_sem=count_recv,
            device_id=(spot_of(turn) * 2 + core, z_to),
            device_id_type=MESH,
        )

    def send_counts(step, unused):
        turn = step // 4
        count_copy(turn, 3 - lax.rem(step, 4)).start()
        return unused

    loads[4].wait()
    ones128 = jnp.ones((128, 128), BF16)

    def lay_asked(chunk):
        arrived = recv.at[pl.ds(max(32 * chunk, 1), 32 if chunk else 31)]
        pltpu.make_async_copy(arrived, arrived, recv_sem.at[chunk]).wait()
        start = chunk * CHUNK
        codes = recv[32 * chunk : 32 * chunk + 32, 0:8, :].reshape(CHUNK, 128)
        lay_codes(codes & 65535, high_asked, low_asked, 0, start)
        lay_codes(codes >> 16, high_asked, low_asked, 1, start)
        slots_in = recv[32 * chunk : 32 * chunk + 32, 8:9, :].reshape(32, 128)
        row_at = iota((CHUNK, 128), 0)
        lane = iota((CHUNK, 128), 1)
        fan = one_hot((iota((CHUNK, 32), 0) >> 3) == iota((CHUNK, 32), 1))
        keep = (row_at & 7) == lane
        slot_high = nn(fan, narrow(slots_in >> 7))
        slot_low = nn(fan, narrow(slots_in & 127))
        slot_high = nn(jnp.where(keep, slot_high, 0.0).astype(BF16), ones128).astype(BF16)
        slot_low = nn(jnp.where(keep, slot_low, 0.0).astype(BF16), ones128).astype(BF16)
        low_hot = jnp.where(slot_low == narrow(lane), one, zero)
        for block in range(CENT_DEV // 128):
            wanted[start : start + CHUNK, block * 128 : (block + 1) * 128] = jnp.where(
                slot_high == jnp.full((), block, BF16), low_hot, zero
            )

    def fetch(block, low_chunk, high_chunk):
        x_to = lax.rem(x + block + 1, 4)
        columns = pl.ds(pl.multiple_of(x_to * 256, 256), 256)
        base = nn(
            wanted[low_chunk * CHUNK : high_chunk * CHUNK, :], table[:, columns]
        ).astype(BF16)
        for chunk in range(low_chunk, high_chunk):
            at = (chunk - low_chunk) * CHUNK
            spread_asked[:, chunk * CHUNK : (chunk + 1) * CHUNK] = nt(
                -eye256, base[at : at + CHUNK]
            ).astype(BF16)

    def add_asked(turn, side, low_chunk, high_chunk):
        spot = spot_of(turn)
        for index in range(2):
            mine = tally(
                spread_asked,
                (lax.rem(spot, 4) * 2 + side) * 32,
                high_asked,
                low_asked,
                spot * 2 + side,
                range(low_chunk, high_chunk),
                index,
            )
            parts[side, turn, :, 2 * index] += mine[:, 0:128].reshape(4, 8, 128)
            parts[side, turn, :, 2 * index + 1] += mine[:, 128:256].reshape(4, 8, 128)

    def early_block(block, unused):
        fetch(block, 0, 1)

        def early_step(step, unused_too):
            for side in range(2):
                add_asked(block * 4 + step, side, 0, 1)
            return unused_too

        lax.fori_loop(0, 4, early_step, 0)
        return unused

    for chunk in range(ASKED // CHUNK):
        lay_asked(chunk)
    count_swap.wait_recv()
    count_half[...] = counts[core] + count_mate[...]
    lax.fori_loop(0, 63, send_counts, 0)

    def core_copy(turn):
        return pltpu.make_async_remote_copy(
            src_ref=parts.at[1 - core, turn],
            dst_ref=mate.at[turn],
            send_sem=core_send.at[turn],
            recv_sem=core_recv.at[turn],
            device_id=mate_id,
            device_id_type=MESH,
        )

    def part_copy(turn, z_step):
        z_to = lax.rem(z + z_step, 4)
        return pltpu.make_async_remote_copy(
            src_ref=half.at[turn, z_to],
            dst_ref=landed.at[turn * 4 + 3 - z_step],
            send_sem=part_send,
            recv_sem=part_recv,
            device_id=(spot_of(turn) * 2 + core, z_to),
            device_id_type=MESH,
        )

    def pass_on(turn):
        core_copy(turn).wait_recv()
        half[turn] = parts[core, turn] + mate[turn]
        for z_step in range(1, 4):
            part_copy(turn, z_step).start()

        @pl.when(turn != 15)
        def _():
            part_copy(turn, 0).start()

    def block_step(block, unused):
        fetch(block, 0, ASKED // CHUNK)

        def spot_step(spot, unused_too):
            turn = block * 4 + spot

            for side in range(2):
                add_asked(turn, side, 0, ASKED // CHUNK)
            core_copy(turn).start()

            @pl.when(turn >= LAG)
            def _():
                pass_on(turn - LAG)

            return unused_too

        lax.fori_loop(0, 4, spot_step, 0)
        return unused

    lax.fori_loop(0, 4, block_step, 0)
    for turn in range(16 - LAG, 16):
        pass_on(jnp.int32(turn))

    others = landed.at[pl.ds(0, 63)]
    pltpu.make_async_copy(others, others, part_recv).wait()

    def add(step, total):
        return total + landed[step]

    total = lax.fori_loop(0, 63, add, half[15, z])
    pltpu.make_async_copy(count_landed, count_landed, count_recv).wait()

    def add_count(step, total):
        return total + count_landed[step]

    count = lax.fori_loop(0, 63, add_count, count_half[15, lax.rem(z, 2)])
    count = jnp.maximum(count, 1.0)
    count_high = jnp.floor(count * (1.0 / 256.0))
    count_low = (count - 256.0 * count_high).astype(BF16)
    count_high = count_high.astype(BF16)
    from_lane = iota((128, 256), 0)
    lane = iota((128, 256), 1)
    sub_lane = ((lane >> 7) * 2 + ((lane >> 3) & 1)) * 16 + (z // 2) * 8 + ((lane >> 4) & 7)
    for index in range(2):
        fan = one_hot(from_lane == index * 64 + sub_lane)
        fanned = 256.0 * nn(count_high, fan) + nn(count_low, fan)
        means[z, 2 * index] = total[2 * index] / fanned[:, 0:128]
        means[z, 2 * index + 1] = total[2 * index + 1] / fanned[:, 128:256]

    for z_step in range(1, 4):
        pltpu.make_async_remote_copy(
            src_ref=means.at[z],
            dst_ref=means.at[z],
            send_sem=last_send,
            recv_sem=last_recv,
            device_id=(rows_at, lax.rem(z + z_step, 4)),
            device_id_type=MESH,
        ).start()
    three = means.at[pl.ds(0, 3)]
    pltpu.make_async_copy(three, three, last_recv).wait()
    for index, out in ((0, out_first), (1, out_second)):
        both = jnp.concatenate(
            [means[:, 2 * index].reshape(32, 128), means[:, 2 * index + 1].reshape(32, 128)], axis=1
        ).T
        out[...] = jnp.concatenate(
            [
                jnp.concatenate([both[16 * v : 16 * v + 16], both[128 + 16 * v : 144 + 16 * v]], axis=0)
                for v in range(8)
            ],
            axis=1,
        )

    pltpu.make_async_copy(three, three, last_send).wait()
    pltpu.make_async_copy(others, others, part_send).wait()
    pltpu.make_async_copy(count_landed, count_landed, count_send).wait()
    count_swap.wait_send()
    rest = send.at[pl.ds(1, DEV - 1)]
    pltpu.make_async_copy(rest, rest, send_sem).wait()

    def end_core(turn, unused):
        core_copy(turn).wait_send()
        return unused

    lax.fori_loop(0, 16, end_core, 0)


def hand_on(first, second, out_first, out_second):
    out_first[...] = first[...]
    out_second[...] = second[...]


def on_device(vectors, list_ids, centroids, list_place, codes_first, codes_second):
    place = list_place.reshape(2048, 128)
    vmem, dma = pltpu.VMEM, pltpu.SemaphoreType.DMA
    first, second = pl.pallas_call(
        kernel,
        out_shape=[jax.ShapeDtypeStruct((32, K), F32)] * 2,
        in_specs=[pl.BlockSpec(memory_space=pltpu.SMEM)]
        + [pl.BlockSpec(memory_space=pl.ANY)] * 5,
        out_specs=[pl.BlockSpec(memory_space=pltpu.VMEM)] * 2,
        scratch_shapes=[
            vmem((2048, 128), I32),
            vmem((ROWS_DEV, S), I32),
            vmem((ROWS_DEV, S), I32),
            vmem((ROWS_DEV, D), BF16),
            vmem((CENT_DEV, D), BF16),
            vmem((ROWS_DEV, 128), I32),
            vmem((DEV, 9, 128), I32),
            vmem((DEV, 9, 128), I32),
            vmem((D, ROWS_DEV), BF16),
            vmem((2, S, ROWS_DEV), F32),
            vmem((2, S, ROWS_DEV), F32),
            vmem((2, S, ROWS_DEV), F32),
            vmem((2, S, ROWS_DEV), F32),
            vmem((ASKED, CENT_DEV), BF16),
            vmem((256, ASKED), BF16),
            vmem((2, S, ASKED), F32),
            vmem((2, S, ASKED), F32),
            vmem((2, 16, 4, 4, 8, 128), F32),
            vmem((16, 4, 4, 8, 128), F32),
            vmem((16, 4, 4, 8, 128), F32),
            vmem((63, 4, 8, 128), F32),
            vmem((2, 16, 2, 8, 128), F32),
            vmem((16, 2, 8, 128), F32),
            vmem((16, 2, 8, 128), F32),
            vmem((63, 8, 128), F32),
            vmem((4, 4, 8, 128), F32),
            dma((5,)),
            dma,
            dma((4,)),
            dma((16,)),
            dma((16,)),
            dma,
            dma,
            dma,
            dma,
            dma,
            dma,
            dma,
            dma,
        ],
        compiler_params=pltpu.CompilerParams(
            collective_id=0, has_side_effects=True, vmem_limit_bytes=60 * 2**20
        ),
        name="codebooks",
    )(list_ids, place, codes_first, codes_second, vectors, centroids)
    first, second = pl.pallas_call(
        hand_on,
        out_shape=[jax.ShapeDtypeStruct((32, K), F32)] * 2,
        in_specs=[pl.BlockSpec(memory_space=vmem)] * 2,
        out_specs=[pl.BlockSpec(memory_space=vmem)] * 2,
        name="hand_on",
    )(first, second)
    return (first.T, second.T)


def solution(mesh):
    return jax.shard_map(
        on_device,
        mesh=mesh,
        in_specs=(
            P(("rows", "rep"), None),
            P(("rows", "rep")),
            P(("rows", "rep"), None),
            P(),
            P(("rows", "rep"), None),
            P(("rows", "rep"), None),
        ),
        out_specs=(P(None, "rows"), P(None, "rows")),
        check_vma=False,
    )
```

```python
import jax
import jax.numpy as jnp
from jax import lax
from jax.experimental import pallas as pl
from jax.experimental.pallas import tpu as pltpu
from jax.sharding import PartitionSpec as P

K = 256
D = 1024
S = 128
DEV = 128
CAP = 8
ROWS_DEV = 512
CENT_DEV = 2048
ASKED = DEV * CAP
CHUNK = 256
LAG = 1
MESH = pl.DeviceIdType.MESH
F32 = jnp.float32
BF16 = jnp.bfloat16
I32 = jnp.int32


def iota(shape, dim):
    return lax.broadcasted_iota(I32, shape, dim)


def nt(a, b):
    return lax.dot_general(a, b, (((1,), (1,)), ((), ())), preferred_element_type=F32)


def nn(a, b):
    return jnp.dot(a, b, preferred_element_type=F32)


def one_hot(match):
    return jnp.where(match, 1.0, 0.0).astype(BF16)


def narrow(whole):
    return whole.astype(F32).astype(BF16)


def kernel(
    ids_hbm,
    place_hbm,
    first_hbm,
    second_hbm,
    vectors_hbm,
    table_hbm,
    out_first,
    out_second,
    ids,
    place,
    first,
    second,
    vectors,
    table,
    found,
    send,
    recv,
    spread_own,
    high_own,
    low_own,
    wanted,
    spread_asked,
    high_asked,
    low_asked,
    parts,
    mate,
    half,
    landed,
    counts,
    count_mate,
    count_half,
    count_landed,
    means,
    load_sem,
    send_sem,
    recv_sem,
    core_send,
    core_recv,
    part_send,
    part_recv,
    swap_send,
    swap_recv,
    count_send,
    count_recv,
    last_send,
    last_recv,
):
    rows_at = lax.axis_index("rows")
    z = lax.axis_index("rep")
    me = rows_at * 4 + z
    core = lax.rem(rows_at, 2)
    y = lax.rem(rows_at // 2, 4)
    x = rows_at // 8
    barrier = pltpu.get_barrier_semaphore()

    loads = []
    for at, (source, target) in enumerate(
        (
            (place_hbm, place),
            (first_hbm, first),
            (second_hbm, second),
            (vectors_hbm, vectors),
            (table_hbm, table),
            (ids_hbm, ids),
        )
    ):
        load = pltpu.make_async_copy(source, target, load_sem.at[at])
        loads.append(load)
    for at in (5, 0, 1, 2):
        loads[at].start()

    def greet(step, unused):
        other = lax.rem(me + step, DEV)
        pl.semaphore_signal(
            barrier, inc=1, device_id=(other // 4, lax.rem(other, 4)), device_id_type=MESH
        )
        return unused

    lax.fori_loop(1, DEV, greet, 0)

    loads[5].wait()
    loads[0].wait()
    loads[3].start()
    loads[4].start()
    lanes = iota((1, 128), 1)

    def find(block, unused):
        for step in range(8):
            row = block * 8 + step
            wish = ids[row]
            found[pl.ds(row, 1), :] = jnp.where(
                lanes == (wish & 127), place[pl.ds(wish >> 7, 1), :], 0
            )
        return unused

    lax.fori_loop(0, ROWS_DEV // 8, find, 0)

    places = found[...]
    ones8 = jnp.ones((8, 128), BF16)
    owner_row = nt(ones8, narrow(places >> 11))[0:1, :].astype(I32)
    slot_high = nt(ones8, narrow((places >> 7) & 15))[0:1, :]
    slot_low = nt(ones8, narrow(places & 127))[0:1, :]
    owner_is = iota((DEV, ROWS_DEV), 0) == owner_row
    owner_hot = one_hot(owner_is)
    earlier = one_hot(iota((ROWS_DEV, ROWS_DEV), 0) < iota((ROWS_DEV, ROWS_DEV), 1))
    before = nn(owner_hot, earlier)
    rank = jnp.sum(jnp.where(owner_is, before, 0.0), axis=0, keepdims=True).astype(I32)
    rank_is = iota((DEV, ROWS_DEV), 0) == rank
    slots_high = nt(owner_hot, jnp.where(rank_is, slot_high, 0.0).astype(BF16))
    slots_low = nt(owner_hot, jnp.where(rank_is, slot_low, 0.0).astype(BF16))
    slots = (slots_high * 128.0 + slots_low).astype(I32)
    position = owner_row * CAP + rank
    loads[1].wait()
    loads[2].wait()
    payload = jnp.concatenate([narrow(first[...] + 1), narrow(second[...] + 1)], axis=1)
    for block in range(4):
        move = one_hot(iota((256, ROWS_DEV), 0) + 256 * block == position)
        moved = nn(move, payload).astype(I32)
        codes = moved[:, 0:128] + moved[:, 128:256] * 65536
        send[32 * block : 32 * block + 32, 0:8, :] = codes.reshape(32, CAP, 128)
    send[:, 8:9, :] = slots.reshape(DEV, 1, 128)

    pl.semaphore_wait(barrier, DEV - 1)

    def push(step, unused):
        other = lax.rem(me + step, DEV)
        pltpu.make_async_remote_copy(
            src_ref=send.at[other],
            dst_ref=recv.at[step],
            send_sem=send_sem,
            recv_sem=recv_sem.at[step >> 5],
            device_id=(other >> 2, other & 3),
            device_id_type=MESH,
        ).start()
        return unused

    lax.fori_loop(1, DEV, push, 0)
    recv[0] = send[me]

    def lay_codes(column, high, low, index, start):
        turned = nt(eye128, narrow(column)) - 1.0
        low_part = jnp.floor(turned * (1.0 / 32.0))
        high_part = turned - 32.0 * low_part
        high[index, :, start : start + CHUNK] = high_part
        low[index, :, start : start + CHUNK] = low_part

    eye128 = one_hot(iota((128, 128), 0) == iota((128, 128), 1))
    eye256 = one_hot(iota((256, 256), 0) == iota((256, 256), 1))

    high_is = narrow(iota((16, CHUNK), 0))
    lane_sub = iota((8, 128), 1) >> 5
    count_is = narrow(iota((16, CHUNK), 0) & 7)
    one = jnp.ones((), BF16)
    zero = jnp.zeros((), BF16)

    def tally(spread, row, high, low, owner, chunks, index, counting):
        total = None
        for chunk in chunks:
            start = chunk * CHUNK
            left, right, mark = [], [], []
            for pair in range(2):
                data = spread[
                    pl.ds(pl.multiple_of(row + 16 * pair, 16), 16), start : start + CHUNK
                ]
                lows = []
                for sub in range(2):
                    at = owner * 4 + pair * 2 + sub
                    h = jnp.broadcast_to(high[index, pl.ds(at, 1), start : start + CHUNK], (8, CHUNK))
                    h = jnp.concatenate([h, h], axis=0).astype(BF16)
                    left.append(jnp.where(h == high_is, one, zero))
                    left.append(jnp.where(h == high_is + 16.0, one, zero))
                    lows.append(
                        jnp.broadcast_to(low[index, pl.ds(at, 1), start : start + CHUNK], (8, CHUNK))
                    )
                l = jnp.concatenate(lows, axis=0).astype(BF16)
                for value in range(8):
                    right.append(jnp.where(l == jnp.full((), value, BF16), data, zero))
                if counting:
                    mark.append(jnp.where(l == count_is, one, zero))
            product = nt(jnp.concatenate(right + mark, axis=0), jnp.concatenate(left, axis=0))
            total = product if total is None else total + product

        def own_lanes(rows):
            mine = total[rows[0] : rows[0] + 8]
            for sub in range(1, 4):
                mine = jnp.where(lane_sub == sub, total[rows[sub] : rows[sub] + 8], mine)
            return mine

        sums = [own_lanes([16 * v, 16 * v + 8, 128 + 16 * v, 136 + 16 * v]) for v in range(8)]
        return sums, own_lanes([256, 264, 272, 280]) if counting else None

    def spot_of(turn):
        x_to = lax.rem(x + turn // 4 + 1, 4)
        y_to = lax.rem(y + lax.rem(turn, 4) + 1, 4)
        return x_to * 4 + y_to

    loads[3].wait()
    for chunk in range(ROWS_DEV // CHUNK):
        start = chunk * CHUNK
        for block in range(D // 256):
            cut = vectors[start : start + CHUNK, block * 256 : (block + 1) * 256]
            spread_own[block * 256 : (block + 1) * 256, start : start + CHUNK] = nt(
                eye256, cut
            ).astype(BF16)
        lay_codes(first[start : start + CHUNK, :] + 1, high_own, low_own, 0, start)
        lay_codes(second[start : start + CHUNK, :] + 1, high_own, low_own, 1, start)

    def own_step(turn, unused):
        for side in range(2):
            owner = spot_of(turn) * 2 + side
            for index in range(2):
                sums, count = tally(
                    spread_own,
                    owner * 32,
                    high_own,
                    low_own,
                    owner,
                    range(ROWS_DEV // CHUNK),
                    index,
                    True,
                )
                for value in range(8):
                    z_of, at = value // 2, 2 * index + value % 2
                    parts[side, turn, z_of, at] = sums[value]
                    counts[side, turn, z_of, at : at + 1, :] = count[value : value + 1]
        return unused


    lax.fori_loop(0, 16, own_step, 0)

    mate_id = (rows_at + 1 - 2 * core, z)
    count_swap = pltpu.make_async_remote_copy(
        src_ref=counts.at[1 - core],
        dst_ref=count_mate,
        send_sem=swap_send,
        recv_sem=swap_recv,
        device_id=mate_id,
        device_id_type=MESH,
    )
    count_swap.start()

    def count_copy(turn, z_step):
        z_to = lax.rem(z + z_step, 4)
        return pltpu.make_async_remote_copy(
            src_ref=count_half.at[turn, z_to],
            dst_ref=count_landed.at[turn * 4 + 3 - z_step],
            send_sem=count_send,
            recv_sem=count_recv,
            device_id=(spot_of(turn) * 2 + core, z_to),
            device_id_type=MESH,
        )

    def send_counts(step, unused):
        turn = step // 4
        count_copy(turn, 3 - lax.rem(step, 4)).start()
        return unused

    loads[4].wait()
    ones128 = jnp.ones((128, 128), BF16)

    def lay_asked(chunk):
        arrived = recv.at[pl.ds(max(32 * chunk, 1), 32 if chunk else 31)]
        pltpu.make_async_copy(arrived, arrived, recv_sem.at[chunk]).wait()
        start = chunk * CHUNK
        codes = recv[32 * chunk : 32 * chunk + 32, 0:8, :].reshape(CHUNK, 128)
        lay_codes(codes & 65535, high_asked, low_asked, 0, start)
        lay_codes(codes >> 16, high_asked, low_asked, 1, start)
        slots_in = recv[32 * chunk : 32 * chunk + 32, 8:9, :].reshape(32, 128)
        row_at = iota((CHUNK, 128), 0)
        lane = iota((CHUNK, 128), 1)
        fan = one_hot((iota((CHUNK, 32), 0) >> 3) == iota((CHUNK, 32), 1))
        keep = (row_at & 7) == lane
        slot_high = nn(fan, narrow(slots_in >> 7))
        slot_low = nn(fan, narrow(slots_in & 127))
        slot_high = nn(jnp.where(keep, slot_high, 0.0).astype(BF16), ones128).astype(BF16)
        slot_low = nn(jnp.where(keep, slot_low, 0.0).astype(BF16), ones128).astype(BF16)
        low_hot = jnp.where(slot_low == narrow(lane), one, zero)
        for block in range(CENT_DEV // 128):
            wanted[start : start + CHUNK, block * 128 : (block + 1) * 128] = jnp.where(
                slot_high == jnp.full((), block, BF16), low_hot, zero
            )

    def fetch(block, low_chunk, high_chunk):
        x_to = lax.rem(x + block + 1, 4)
        columns = pl.ds(pl.multiple_of(x_to * 256, 256), 256)
        base = nn(
            wanted[low_chunk * CHUNK : high_chunk * CHUNK, :], table[:, columns]
        ).astype(BF16)
        for chunk in range(low_chunk, high_chunk):
            at = (chunk - low_chunk) * CHUNK
            spread_asked[:, chunk * CHUNK : (chunk + 1) * CHUNK] = nt(
                -eye256, base[at : at + CHUNK]
            ).astype(BF16)

    def add_asked(turn, side, low_chunk, high_chunk):
        spot = spot_of(turn)
        for index in range(2):
            sums, unused_count = tally(
                spread_asked,
                (lax.rem(spot, 4) * 2 + side) * 32,
                high_asked,
                low_asked,
                spot * 2 + side,
                range(low_chunk, high_chunk),
                index,
                False,
            )
            for value in range(8):
                parts[side, turn, value // 2, 2 * index + value % 2] += sums[value]

    def early_block(block, unused):
        fetch(block, 0, 1)

        def early_step(step, unused_too):
            for side in range(2):
                add_asked(block * 4 + step, side, 0, 1)
            return unused_too

        lax.fori_loop(0, 4, early_step, 0)
        return unused

    for chunk in range(ASKED // CHUNK):
        lay_asked(chunk)

    def core_copy(turn):
        return pltpu.make_async_remote_copy(
            src_ref=parts.at[1 - core, turn],
            dst_ref=mate.at[turn],
            send_sem=core_send.at[turn],
            recv_sem=core_recv.at[turn],
            device_id=mate_id,
            device_id_type=MESH,
        )

    def part_copy(turn, z_step):
        z_to = lax.rem(z + z_step, 4)
        return pltpu.make_async_remote_copy(
            src_ref=half.at[turn, z_to],
            dst_ref=landed.at[turn * 4 + 3 - z_step],
            send_sem=part_send,
            recv_sem=part_recv,
            device_id=(spot_of(turn) * 2 + core, z_to),
            device_id_type=MESH,
        )

    def pass_on(turn):
        core_copy(turn).wait_recv()
        half[turn] = parts[core, turn] + mate[turn]
        for z_step in range(1, 4):
            part_copy(turn, z_step).start()

        @pl.when(turn != 15)
        def _():
            part_copy(turn, 0).start()

    def block_step(block, unused):
        fetch(block, 0, ASKED // CHUNK)

        @pl.when(block == 1)
        def _():
            count_swap.wait_recv()
            count_half[...] = counts[core] + count_mate[...]
            lax.fori_loop(0, 63, send_counts, 0)


        def spot_step(spot, unused_too):
            turn = block * 4 + spot

            for side in range(2):
                add_asked(turn, side, 0, ASKED // CHUNK)
            core_copy(turn).start()

            @pl.when(turn >= LAG)
            def _():
                pass_on(turn - LAG)

            return unused_too

        lax.fori_loop(0, 4, spot_step, 0)
        return unused

    lax.fori_loop(0, 4, block_step, 0)
    for turn in range(16 - LAG, 16):
        pass_on(jnp.int32(turn))

    others = landed.at[pl.ds(0, 63)]
    pltpu.make_async_copy(others, others, part_recv).wait()

    def add(step, total):
        return total + landed[step]

    total = lax.fori_loop(0, 63, add, half[15, z])
    pltpu.make_async_copy(count_landed, count_landed, count_recv).wait()

    def add_count(step, total):
        return total + count_landed[step]

    count = lax.fori_loop(0, 63, add_count, count_half[15, z])
    count = jnp.maximum(count, 1.0)
    for at in range(4):
        means[z, at] = total[at] / count[at : at + 1, :]

    for z_step in range(1, 4):
        pltpu.make_async_remote_copy(
            src_ref=means.at[z],
            dst_ref=means.at[z],
            send_sem=last_send,
            recv_sem=last_recv,
            device_id=(rows_at, lax.rem(z + z_step, 4)),
            device_id_type=MESH,
        ).start()
    three = means.at[pl.ds(0, 3)]
    pltpu.make_async_copy(three, three, last_recv).wait()
    for index, out in ((0, out_first), (1, out_second)):
        for sub in range(4):
            out[8 * sub : 8 * sub + 8, :] = jnp.concatenate(
                [
                    means[v // 2, 2 * index + v % 2][:, 32 * sub : 32 * sub + 32]
                    for v in range(8)
                ],
                axis=1,
            )

    pltpu.make_async_copy(three, three, last_send).wait()
    pltpu.make_async_copy(others, others, part_send).wait()
    pltpu.make_async_copy(count_landed, count_landed, count_send).wait()
    count_swap.wait_send()
    rest = send.at[pl.ds(1, DEV - 1)]
    pltpu.make_async_copy(rest, rest, send_sem).wait()

    def end_core(turn, unused):
        core_copy(turn).wait_send()
        return unused

    lax.fori_loop(0, 16, end_core, 0)


def hand_on(first, second, out_first, out_second):
    out_first[...] = first[...]
    out_second[...] = second[...]


def on_device(vectors, list_ids, centroids, list_place, codes_first, codes_second):
    place = list_place.reshape(2048, 128)
    vmem, dma = pltpu.VMEM, pltpu.SemaphoreType.DMA
    first, second = pl.pallas_call(
        kernel,
        out_shape=[jax.ShapeDtypeStruct((32, K), F32)] * 2,
        in_specs=[pl.BlockSpec(memory_space=pl.ANY)] * 6,
        out_specs=[pl.BlockSpec(memory_space=pltpu.VMEM)] * 2,
        scratch_shapes=[
            pltpu.SMEM((ROWS_DEV,), I32),
            vmem((2048, 128), I32),
            vmem((ROWS_DEV, S), I32),
            vmem((ROWS_DEV, S), I32),
            vmem((ROWS_DEV, D), BF16),
            vmem((CENT_DEV, D), BF16),
            vmem((ROWS_DEV, 128), I32),
            vmem((DEV, 9, 128), I32),
            vmem((DEV, 9, 128), I32),
            vmem((D, ROWS_DEV), BF16),
            vmem((2, S, ROWS_DEV), F32),
            vmem((2, S, ROWS_DEV), F32),
            vmem((ASKED, CENT_DEV), BF16),
            vmem((256, ASKED), BF16),
            vmem((2, S, ASKED), F32),
            vmem((2, S, ASKED), F32),
            vmem((2, 16, 4, 4, 8, 128), F32),
            vmem((16, 4, 4, 8, 128), F32),
            vmem((16, 4, 4, 8, 128), F32),
            vmem((63, 4, 8, 128), F32),
            vmem((2, 16, 4, 4, 128), F32),
            vmem((16, 4, 4, 128), F32),
            vmem((16, 4, 4, 128), F32),
            vmem((63, 4, 128), F32),
            vmem((4, 4, 8, 128), F32),
            dma((6,)),
            dma,
            dma((4,)),
            dma((16,)),
            dma((16,)),
            dma,
            dma,
            dma,
            dma,
            dma,
            dma,
            dma,
            dma,
        ],
        compiler_params=pltpu.CompilerParams(
            collective_id=0, has_side_effects=True, vmem_limit_bytes=60 * 2**20
        ),
        name="codebooks",
    )(list_ids, place, codes_first, codes_second, vectors, centroids)
    first, second = pl.pallas_call(
        hand_on,
        out_shape=[jax.ShapeDtypeStruct((32, K), F32)] * 2,
        in_specs=[pl.BlockSpec(memory_space=vmem)] * 2,
        out_specs=[pl.BlockSpec(memory_space=vmem)] * 2,
        name="hand_on",
    )(first, second)
    return (first.T, second.T)


def solution(mesh):
    return jax.shard_map(
        on_device,
        mesh=mesh,
        in_specs=(
            P(("rows", "rep"), None),
            P(("rows", "rep")),
            P(("rows", "rep"), None),
            P(),
            P(("rows", "rep"), None),
            P(("rows", "rep"), None),
        ),
        out_specs=(P(None, "rows"), P(None, "rows")),
        check_vma=False,
    )
```

```python
import jax
import jax.numpy as jnp
from jax import lax
from jax.experimental import pallas as pl
from jax.experimental.pallas import tpu as pltpu
from jax.sharding import PartitionSpec as P

K = 256
D = 1024
S = 128
DEV = 128
CAP = 8
ROWS_DEV = 512
CENT_DEV = 2048
ASKED = DEV * CAP
CHUNK = 256
WIDE = 512
LAG = 2
SPLIT = 12
MESH = pl.DeviceIdType.MESH
F32 = jnp.float32
BF16 = jnp.bfloat16
I32 = jnp.int32


def iota(shape, dim):
    return lax.broadcasted_iota(I32, shape, dim)


def nt(a, b):
    return lax.dot_general(a, b, (((1,), (1,)), ((), ())), preferred_element_type=F32)


def nn(a, b):
    return jnp.dot(a, b, preferred_element_type=F32)


def one_hot(match):
    return jnp.where(match, 1.0, 0.0).astype(BF16)


def narrow(whole):
    return whole.astype(F32).astype(BF16)


def kernel(
    ids_hbm,
    place_hbm,
    first_hbm,
    second_hbm,
    vectors_hbm,
    table_hbm,
    out_first,
    out_second,
    ids,
    place,
    first,
    second,
    vectors,
    table,
    found,
    earlier,
    send,
    recv,
    spread_own,
    high_own,
    low_own,
    wanted,
    spread_asked,
    high_asked,
    low_asked,
    parts,
    mate,
    half,
    landed,
    counts,
    count_mate,
    count_half,
    count_landed,
    means,
    load_sem,
    send_sem,
    recv_sem,
    core_send,
    core_recv,
    part_send,
    part_recv,
    swap_send,
    swap_recv,
    count_send,
    count_recv,
    last_send,
    last_recv,
):
    rows_at = lax.axis_index("rows")
    z = lax.axis_index("rep")
    me = rows_at * 4 + z
    core = lax.rem(rows_at, 2)
    y = lax.rem(rows_at // 2, 4)
    x = rows_at // 8
    barrier = pltpu.get_barrier_semaphore()

    loads = []
    for at, (source, target) in enumerate(
        (
            (place_hbm, place),
            (first_hbm, first),
            (second_hbm, second),
            (vectors_hbm, vectors),
            (table_hbm, table),
            (ids_hbm, ids),
        )
    ):
        load = pltpu.make_async_copy(source, target, load_sem.at[at])
        loads.append(load)
    for at in (5, 0, 1, 2):
        loads[at].start()

    def greet(step, unused):
        other = lax.rem(me + step, DEV)
        pl.semaphore_signal(
            barrier, inc=1, device_id=(other // 4, lax.rem(other, 4)), device_id_type=MESH
        )
        return unused

    lax.fori_loop(1, DEV, greet, 0)

    earlier[...] = one_hot(iota((ROWS_DEV, ROWS_DEV), 0) < iota((ROWS_DEV, ROWS_DEV), 1))

    loads[5].wait()
    loads[0].wait()
    loads[3].start()
    loads[4].start()
    lanes = iota((1, 128), 1)

    def find(block, unused):
        for step in range(8):
            row = block * 8 + step
            wish = ids[row]
            found[pl.ds(row, 1), :] = jnp.where(
                lanes == (wish & 127), place[pl.ds(wish >> 7, 1), :], 0
            )
        return unused

    lax.fori_loop(0, ROWS_DEV // 8, find, 0)

    places = found[...]
    ones8 = jnp.ones((8, 128), BF16)
    owner_row = nt(ones8, narrow(places >> 11))[0:1, :].astype(I32)
    slot_high = nt(ones8, narrow((places >> 7) & 15))[0:1, :]
    slot_low = nt(ones8, narrow(places & 127))[0:1, :]
    owner_is = iota((DEV, ROWS_DEV), 0) == owner_row
    owner_hot = one_hot(owner_is)
    before = nn(owner_hot, earlier[...])
    rank = jnp.sum(jnp.where(owner_is, before, 0.0), axis=0, keepdims=True).astype(I32)
    rank_is = iota((DEV, ROWS_DEV), 0) == rank
    slots_high = nt(owner_hot, jnp.where(rank_is, slot_high, 0.0).astype(BF16))
    slots_low = nt(owner_hot, jnp.where(rank_is, slot_low, 0.0).astype(BF16))
    slots = (slots_high * 128.0 + slots_low).astype(I32)
    position = owner_row * CAP + rank
    loads[1].wait()
    loads[2].wait()
    payload = jnp.concatenate([narrow(first[...] + 1), narrow(second[...] + 1)], axis=1)
    for block in range(4):
        move = one_hot(iota((256, ROWS_DEV), 0) + 256 * block == position)
        moved = nn(move, payload).astype(I32)
        codes = moved[:, 0:128] + moved[:, 128:256] * 65536
        send[32 * block : 32 * block + 32, 0:8, :] = codes.reshape(32, CAP, 128)
    send[:, 8:9, :] = slots.reshape(DEV, 1, 128)

    pl.semaphore_wait(barrier, DEV - 1)

    def push(step, unused):
        other = lax.rem(me + step, DEV)
        pltpu.make_async_remote_copy(
            src_ref=send.at[other],
            dst_ref=recv.at[step],
            send_sem=send_sem,
            recv_sem=recv_sem.at[step >> 5],
            device_id=(other >> 2, other & 3),
            device_id_type=MESH,
        ).start()
        return unused

    lax.fori_loop(1, DEV, push, 0)
    recv[0] = send[me]

    def lay_codes(column, high, low, index, start):
        turned = nt(eye128, narrow(column)) - 1.0
        low_part = jnp.floor(turned * (1.0 / 32.0))
        high_part = turned - 32.0 * low_part
        high[index, :, start : start + CHUNK] = high_part
        low[index, :, start : start + CHUNK] = low_part

    eye128 = one_hot(iota((128, 128), 0) == iota((128, 128), 1))
    eye256 = one_hot(iota((256, 256), 0) == iota((256, 256), 1))

    high_is = narrow(iota((16, WIDE), 0))
    lane_sub = iota((8, 128), 1) >> 5
    count_is = narrow(iota((16, WIDE), 0) & 7)
    one = jnp.ones((), BF16)
    zero = jnp.zeros((), BF16)

    def tally(spread, row, high, low, owner, chunks, index, counting):
        total = None
        for chunk in chunks:
            start = chunk * WIDE
            left, right, mark = [], [], []
            for pair in range(2):
                data = spread[
                    pl.ds(pl.multiple_of(row + 16 * pair, 16), 16), start : start + WIDE
                ]
                lows = []
                for sub in range(2):
                    at = owner * 4 + pair * 2 + sub
                    h = jnp.broadcast_to(high[index, pl.ds(at, 1), start : start + WIDE], (8, WIDE))
                    h = jnp.concatenate([h, h], axis=0).astype(BF16)
                    left.append(jnp.where(h == high_is, one, zero))
                    left.append(jnp.where(h == high_is + 16.0, one, zero))
                    lows.append(
                        jnp.broadcast_to(low[index, pl.ds(at, 1), start : start + WIDE], (8, WIDE))
                    )
                l = jnp.concatenate(lows, axis=0).astype(BF16)
                for value in range(8):
                    right.append(jnp.where(l == jnp.full((), value, BF16), data, zero))
                if counting:
                    mark.append(jnp.where(l == count_is, one, zero))
            product = nt(jnp.concatenate(right + mark, axis=0), jnp.concatenate(left, axis=0))
            total = product if total is None else total + product

        def own_lanes(rows):
            mine = total[rows[0] : rows[0] + 8]
            for sub in range(1, 4):
                mine = jnp.where(lane_sub == sub, total[rows[sub] : rows[sub] + 8], mine)
            return mine

        sums = [own_lanes([16 * v, 16 * v + 8, 128 + 16 * v, 136 + 16 * v]) for v in range(8)]
        return sums, own_lanes([256, 264, 272, 280]) if counting else None

    def spot_of(turn):
        x_to = lax.rem(x + turn // 4 + 1, 4)
        y_to = lax.rem(y + lax.rem(turn, 4) + 1, 4)
        return x_to * 4 + y_to

    loads[3].wait()
    for chunk in range(ROWS_DEV // CHUNK):
        start = chunk * CHUNK
        for block in range(D // 256):
            cut = vectors[start : start + CHUNK, block * 256 : (block + 1) * 256]
            spread_own[block * 256 : (block + 1) * 256, start : start + CHUNK] = nt(
                eye256, cut
            ).astype(BF16)
        lay_codes(first[start : start + CHUNK, :] + 1, high_own, low_own, 0, start)
        lay_codes(second[start : start + CHUNK, :] + 1, high_own, low_own, 1, start)

    def own_step(turn, unused):
        for side in range(2):
            owner = spot_of(turn) * 2 + side
            for index in range(2):
                sums, count = tally(
                    spread_own,
                    owner * 32,
                    high_own,
                    low_own,
                    owner,
                    range(ROWS_DEV // WIDE),
                    index,
                    True,
                )
                for value in range(8):
                    z_of, at = value // 2, 2 * index + value % 2
                    parts[side, turn, z_of, at] = sums[value]
                    counts[side, turn, z_of, at : at + 1, :] = count[value : value + 1]
        return unused


    lax.fori_loop(0, 16, own_step, 0)

    mate_id = (rows_at + 1 - 2 * core, z)
    count_swap = pltpu.make_async_remote_copy(
        src_ref=counts.at[1 - core],
        dst_ref=count_mate,
        send_sem=swap_send,
        recv_sem=swap_recv,
        device_id=mate_id,
        device_id_type=MESH,
    )
    count_swap.start()

    def count_copy(turn, z_step):
        z_to = lax.rem(z + z_step, 4)
        return pltpu.make_async_remote_copy(
            src_ref=count_half.at[turn, z_to],
            dst_ref=count_landed.at[turn * 4 + 3 - z_step],
            send_sem=count_send,
            recv_sem=count_recv,
            device_id=(spot_of(turn) * 2 + core, z_to),
            device_id_type=MESH,
        )

    def send_counts(step, unused):
        turn = step // 4
        count_copy(turn, 3 - lax.rem(step, 4)).start()
        return unused

    loads[4].wait()
    ones128 = jnp.ones((128, 128), BF16)

    def lay_asked(chunk):
        arrived = recv.at[pl.ds(max(32 * chunk, 1), 32 if chunk else 31)]
        pltpu.make_async_copy(arrived, arrived, recv_sem.at[chunk]).wait()
        start = chunk * CHUNK
        codes = recv[32 * chunk : 32 * chunk + 32, 0:8, :].reshape(CHUNK, 128)
        lay_codes(codes & 65535, high_asked, low_asked, 0, start)
        lay_codes(codes >> 16, high_asked, low_asked, 1, start)
        slots_in = recv[32 * chunk : 32 * chunk + 32, 8:9, :].reshape(32, 128)
        row_at = iota((CHUNK, 128), 0)
        lane = iota((CHUNK, 128), 1)
        fan = one_hot((iota((CHUNK, 32), 0) >> 3) == iota((CHUNK, 32), 1))
        keep = (row_at & 7) == lane
        slot_high = nn(fan, narrow(slots_in >> 7))
        slot_low = nn(fan, narrow(slots_in & 127))
        slot_high = nn(jnp.where(keep, slot_high, 0.0).astype(BF16), ones128).astype(BF16)
        slot_low = nn(jnp.where(keep, slot_low, 0.0).astype(BF16), ones128).astype(BF16)
        low_hot = jnp.where(slot_low == narrow(lane), one, zero)
        for block in range(CENT_DEV // 128):
            wanted[start : start + CHUNK, block * 128 : (block + 1) * 128] = jnp.where(
                slot_high == jnp.full((), block, BF16), low_hot, zero
            )

    def fetch(block, low_chunk, high_chunk):
        x_to = lax.rem(x + block + 1, 4)
        columns = pl.ds(pl.multiple_of(x_to * 256, 256), 256)
        base = nn(
            wanted[low_chunk * CHUNK : high_chunk * CHUNK, :], table[:, columns]
        ).astype(BF16)
        for chunk in range(low_chunk, high_chunk):
            at = (chunk - low_chunk) * CHUNK
            spread_asked[:, chunk * CHUNK : (chunk + 1) * CHUNK] = nt(
                -eye256, base[at : at + CHUNK]
            ).astype(BF16)

    def add_asked(turn, side, low_chunk, high_chunk):
        spot = spot_of(turn)
        for index in range(2):
            sums, unused_count = tally(
                spread_asked,
                (lax.rem(spot, 4) * 2 + side) * 32,
                high_asked,
                low_asked,
                spot * 2 + side,
                range(low_chunk * CHUNK // WIDE, high_chunk * CHUNK // WIDE),
                index,
                False,
            )
            for value in range(8):
                parts[side, turn, value // 2, 2 * index + value % 2] += sums[value]

    def early_block(block, unused):
        fetch(block, 0, 1)

        def early_step(step, unused_too):
            for side in range(2):
                add_asked(block * 4 + step, side, 0, 1)
            return unused_too

        lax.fori_loop(0, 4, early_step, 0)
        return unused

    for chunk in range(ASKED // CHUNK):
        lay_asked(chunk)

    def core_copy(turn):
        return pltpu.make_async_remote_copy(
            src_ref=parts.at[1 - core, turn],
            dst_ref=mate.at[turn],
            send_sem=core_send.at[turn],
            recv_sem=core_recv.at[turn],
            device_id=mate_id,
            device_id_type=MESH,
        )

    def part_copy(turn, z_step):
        z_to = lax.rem(z + z_step, 4)
        return pltpu.make_async_remote_copy(
            src_ref=half.at[turn, z_to],
            dst_ref=landed.at[turn * 4 + 3 - z_step],
            send_sem=part_send,
            recv_sem=part_recv.at[turn // SPLIT],
            device_id=(spot_of(turn) * 2 + core, z_to),
            device_id_type=MESH,
        )

    def pass_on(turn):
        core_copy(turn).wait_recv()
        half[turn] = parts[core, turn] + mate[turn]
        for z_step in range(1, 4):
            part_copy(turn, z_step).start()

        @pl.when(turn != 15)
        def _():
            part_copy(turn, 0).start()

    def block_step(block, unused):
        fetch(block, 0, ASKED // CHUNK)

        @pl.when(block == 1)
        def _():
            count_swap.wait_recv()
            count_half[...] = counts[core] + count_mate[...]
            lax.fori_loop(0, 63, send_counts, 0)


        def spot_step(spot, unused_too):
            turn = block * 4 + spot

            for side in range(2):
                add_asked(turn, side, 0, ASKED // CHUNK)
            core_copy(turn).start()

            @pl.when(turn >= LAG)
            def _():
                pass_on(turn - LAG)

            return unused_too

        lax.fori_loop(0, 4, spot_step, 0)
        return unused

    lax.fori_loop(0, 4, block_step, 0)
    for turn in range(16 - LAG, 16):
        pass_on(jnp.int32(turn))

    pltpu.make_async_copy(count_landed, count_landed, count_recv).wait()
    count = count_half[15, z]
    for step in range(63):
        count = count + count_landed[step]
    count = jnp.maximum(count, 1.0)

    total = half[15, z]
    for group, (begin, end) in enumerate(((0, 4 * SPLIT), (4 * SPLIT, 63))):
        others = landed.at[pl.ds(begin, end - begin)]
        pltpu.make_async_copy(others, others, part_recv.at[group]).wait()
        for step in range(begin, end):
            total = total + landed[step]

    for at in range(4):
        means[z, at] = total[at] / count[at : at + 1, :]

    for z_step in range(1, 4):
        pltpu.make_async_remote_copy(
            src_ref=means.at[z],
            dst_ref=means.at[z],
            send_sem=last_send,
            recv_sem=last_recv,
            device_id=(rows_at, lax.rem(z + z_step, 4)),
            device_id_type=MESH,
        ).start()
    all_landed = landed.at[pl.ds(0, 63)]
    pltpu.make_async_copy(all_landed, all_landed, part_send).wait()
    pltpu.make_async_copy(count_landed, count_landed, count_send).wait()
    count_swap.wait_send()
    rest = send.at[pl.ds(1, DEV - 1)]
    pltpu.make_async_copy(rest, rest, send_sem).wait()

    def end_core(turn, unused):
        core_copy(turn).wait_send()
        return unused

    lax.fori_loop(0, 16, end_core, 0)
    three = means.at[pl.ds(0, 3)]
    pltpu.make_async_copy(three, three, last_send).wait()
    pltpu.make_async_copy(three, three, last_recv).wait()
    for index, out in ((0, out_first), (1, out_second)):
        for sub in range(4):
            out[8 * sub : 8 * sub + 8, :] = jnp.concatenate(
                [
                    means[v // 2, 2 * index + v % 2][:, 32 * sub : 32 * sub + 32]
                    for v in range(8)
                ],
                axis=1,
            )


def hand_on(first, second, out_first, out_second):
    out_first[...] = first[...]
    out_second[...] = second[...]


def on_device(vectors, list_ids, centroids, list_place, codes_first, codes_second):
    place = list_place.reshape(2048, 128)
    vmem, dma = pltpu.VMEM, pltpu.SemaphoreType.DMA
    first, second = pl.pallas_call(
        kernel,
        out_shape=[jax.ShapeDtypeStruct((32, K), F32)] * 2,
        in_specs=[pl.BlockSpec(memory_space=pl.ANY)] * 6,
        out_specs=[pl.BlockSpec(memory_space=pltpu.VMEM)] * 2,
        scratch_shapes=[
            pltpu.SMEM((ROWS_DEV,), I32),
            vmem((2048, 128), I32),
            vmem((ROWS_DEV, S), I32),
            vmem((ROWS_DEV, S), I32),
            vmem((ROWS_DEV, D), BF16),
            vmem((CENT_DEV, D), BF16),
            vmem((ROWS_DEV, 128), I32),
            vmem((ROWS_DEV, ROWS_DEV), BF16),
            vmem((DEV, 9, 128), I32),
            vmem((DEV, 9, 128), I32),
            vmem((D, ROWS_DEV), BF16),
            vmem((2, S, ROWS_DEV), F32),
            vmem((2, S, ROWS_DEV), F32),
            vmem((ASKED, CENT_DEV), BF16),
            vmem((256, ASKED), BF16),
            vmem((2, S, ASKED), F32),
            vmem((2, S, ASKED), F32),
            vmem((2, 16, 4, 4, 8, 128), F32),
            vmem((16, 4, 4, 8, 128), F32),
            vmem((16, 4, 4, 8, 128), F32),
            vmem((63, 4, 8, 128), F32),
            vmem((2, 16, 4, 4, 128), F32),
            vmem((16, 4, 4, 128), F32),
            vmem((16, 4, 4, 128), F32),
            vmem((63, 4, 128), F32),
            vmem((4, 4, 8, 128), F32),
            dma((6,)),
            dma,
            dma((4,)),
            dma((16,)),
            dma((16,)),
            dma,
            dma((2,)),
            dma,
            dma,
            dma,
            dma,
            dma,
            dma,
        ],
        compiler_params=pltpu.CompilerParams(
            collective_id=0, has_side_effects=True, vmem_limit_bytes=60 * 2**20
        ),
        name="codebooks",
    )(list_ids, place, codes_first, codes_second, vectors, centroids)
    first, second = pl.pallas_call(
        hand_on,
        out_shape=[jax.ShapeDtypeStruct((32, K), F32)] * 2,
        in_specs=[pl.BlockSpec(memory_space=vmem)] * 2,
        out_specs=[pl.BlockSpec(memory_space=vmem)] * 2,
        name="hand_on",
    )(first, second)
    return (first.T, second.T)


def solution(mesh):
    return jax.shard_map(
        on_device,
        mesh=mesh,
        in_specs=(
            P(("rows", "rep"), None),
            P(("rows", "rep")),
            P(("rows", "rep"), None),
            P(),
            P(("rows", "rep"), None),
            P(("rows", "rep"), None),
        ),
        out_specs=(P(None, "rows"), P(None, "rows")),
        check_vma=False,
    )
```

```python
import jax
import jax.numpy as jnp
from jax import lax
from jax.experimental import pallas as pl
from jax.experimental.pallas import tpu as pltpu
from jax.sharding import PartitionSpec as P

K = 256
D = 1024
S = 128
DEV = 128
CAP = 8
ROWS_DEV = 512
CENT_DEV = 2048
ASKED = DEV * CAP
CHUNK = 256
WIDE = 512
LAG = 2
SPLIT = 12
MESH = pl.DeviceIdType.MESH
F32 = jnp.float32
BF16 = jnp.bfloat16
I32 = jnp.int32


def iota(shape, dim):
    return lax.broadcasted_iota(I32, shape, dim)


def nt(a, b):
    return lax.dot_general(a, b, (((1,), (1,)), ((), ())), preferred_element_type=F32)


def nn(a, b):
    return jnp.dot(a, b, preferred_element_type=F32)


def one_hot(match):
    return jnp.where(match, 1.0, 0.0).astype(BF16)


def narrow(whole):
    return whole.astype(F32).astype(BF16)


def kernel(
    ids_hbm,
    place_hbm,
    first_hbm,
    second_hbm,
    vectors_hbm,
    table_hbm,
    out_first,
    out_second,
    ids,
    place,
    first,
    second,
    vectors,
    table,
    found,
    earlier,
    send,
    recv,
    spread_own,
    high_own,
    low_own,
    wanted,
    spread_asked,
    high_asked,
    low_asked,
    parts,
    mate,
    half,
    landed,
    counts,
    count_mate,
    count_half,
    count_landed,
    means,
    load_sem,
    send_sem,
    recv_sem,
    core_send,
    core_recv,
    part_send,
    part_recv,
    swap_send,
    swap_recv,
    count_send,
    count_recv,
    last_send,
    last_recv,
):
    rows_at = lax.axis_index("rows")
    z = lax.axis_index("rep")
    me = rows_at * 4 + z
    core = lax.rem(rows_at, 2)
    y = lax.rem(rows_at // 2, 4)
    x = rows_at // 8
    barrier = pltpu.get_barrier_semaphore()

    loads = []
    for at, (source, target) in enumerate(
        (
            (place_hbm, place),
            (first_hbm, first),
            (second_hbm, second),
            (vectors_hbm, vectors),
            (table_hbm, table),
            (ids_hbm, ids),
        )
    ):
        load = pltpu.make_async_copy(source, target, load_sem.at[at])
        loads.append(load)
    for at in (5, 0, 1, 2):
        loads[at].start()

    def greet(step, unused):
        other = lax.rem(me + step, DEV)
        pl.semaphore_signal(
            barrier, inc=1, device_id=(other // 4, lax.rem(other, 4)), device_id_type=MESH
        )
        return unused

    lax.fori_loop(1, DEV, greet, 0)

    earlier[...] = one_hot(iota((ROWS_DEV, ROWS_DEV), 0) < iota((ROWS_DEV, ROWS_DEV), 1))

    loads[5].wait()
    loads[0].wait()
    loads[3].start()
    loads[4].start()
    lanes = iota((1, 128), 1)

    def find(block, unused):
        for step in range(8):
            row = block * 8 + step
            wish = ids[row]
            found[pl.ds(row, 1), :] = jnp.where(
                lanes == (wish & 127), place[pl.ds(wish >> 7, 1), :], 0
            )
        return unused

    lax.fori_loop(0, ROWS_DEV // 8, find, 0)

    places = found[...]
    ones8 = jnp.ones((8, 128), BF16)
    owner_row = nt(ones8, narrow(places >> 11))[0:1, :].astype(I32)
    slot_high = nt(ones8, narrow((places >> 7) & 15))[0:1, :]
    slot_low = nt(ones8, narrow(places & 127))[0:1, :]
    owner_is = iota((DEV, ROWS_DEV), 0) == owner_row
    owner_hot = one_hot(owner_is)
    before = nn(owner_hot, earlier[...])
    rank = jnp.sum(jnp.where(owner_is, before, 0.0), axis=0, keepdims=True).astype(I32)
    rank_is = iota((DEV, ROWS_DEV), 0) == rank
    slots_high = nt(owner_hot, jnp.where(rank_is, slot_high, 0.0).astype(BF16))
    slots_low = nt(owner_hot, jnp.where(rank_is, slot_low, 0.0).astype(BF16))
    slots = (slots_high * 128.0 + slots_low).astype(I32)
    position = owner_row * CAP + rank
    loads[1].wait()
    loads[2].wait()
    payload = jnp.concatenate([narrow(first[...] + 1), narrow(second[...] + 1)], axis=1)
    for block in range(4):
        move = one_hot(iota((256, ROWS_DEV), 0) + 256 * block == position)
        moved = nn(move, payload).astype(I32)
        codes = moved[:, 0:128] + moved[:, 128:256] * 65536
        send[32 * block : 32 * block + 32, 0:8, :] = codes.reshape(32, CAP, 128)
    send[:, 8:9, :] = slots.reshape(DEV, 1, 128)

    pl.semaphore_wait(barrier, DEV - 1)

    def push(step, unused):
        other = lax.rem(me + step, DEV)
        pltpu.make_async_remote_copy(
            src_ref=send.at[other],
            dst_ref=recv.at[step],
            send_sem=send_sem,
            recv_sem=recv_sem.at[step >> 5],
            device_id=(other >> 2, other & 3),
            device_id_type=MESH,
        ).start()
        return unused

    lax.fori_loop(1, DEV, push, 0)
    recv[0] = send[me]

    def lay_codes(column, high, low, index, start):
        turned = nt(eye128, narrow(column)) - 1.0
        low_part = jnp.floor(turned * (1.0 / 32.0))
        high_part = turned - 32.0 * low_part
        high[index, :, start : start + CHUNK] = high_part
        low[index, :, start : start + CHUNK] = low_part

    eye128 = one_hot(iota((128, 128), 0) == iota((128, 128), 1))
    eye256 = one_hot(iota((256, 256), 0) == iota((256, 256), 1))

    high_is = narrow(iota((16, WIDE), 0))
    lane_sub = iota((8, 128), 1) >> 5
    count_is = narrow(iota((16, WIDE), 0) & 7)
    one = jnp.ones((), BF16)
    zero = jnp.zeros((), BF16)

    def tally(spread, row, high, low, owner, chunks, index, counting):
        total = None
        for chunk in chunks:
            start = chunk * WIDE
            left, right, mark = [], [], []
            for pair in range(2):
                data = spread[
                    pl.ds(pl.multiple_of(row + 16 * pair, 16), 16), start : start + WIDE
                ]
                lows = []
                for sub in range(2):
                    at = owner * 4 + pair * 2 + sub
                    h = jnp.broadcast_to(high[index, pl.ds(at, 1), start : start + WIDE], (8, WIDE))
                    h = jnp.concatenate([h, h], axis=0).astype(BF16)
                    left.append(jnp.where(h == high_is, one, zero))
                    left.append(jnp.where(h == high_is + 16.0, one, zero))
                    lows.append(
                        jnp.broadcast_to(low[index, pl.ds(at, 1), start : start + WIDE], (8, WIDE))
                    )
                l = jnp.concatenate(lows, axis=0).astype(BF16)
                for value in range(8):
                    right.append(jnp.where(l == jnp.full((), value, BF16), data, zero))
                if counting:
                    mark.append(jnp.where(l == count_is, one, zero))
            product = nt(jnp.concatenate(right + mark, axis=0), jnp.concatenate(left, axis=0))
            total = product if total is None else total + product

        def own_lanes(rows):
            mine = total[rows[0] : rows[0] + 8]
            for sub in range(1, 4):
                mine = jnp.where(lane_sub == sub, total[rows[sub] : rows[sub] + 8], mine)
            return mine

        sums = [own_lanes([16 * v, 16 * v + 8, 128 + 16 * v, 136 + 16 * v]) for v in range(8)]
        return sums, own_lanes([256, 264, 272, 280]) if counting else None

    def spot_of(turn):
        x_to = lax.rem(x + turn // 4 + 1, 4)
        y_to = lax.rem(y + lax.rem(turn, 4) + 1, 4)
        return x_to * 4 + y_to

    loads[3].wait()
    for chunk in range(ROWS_DEV // CHUNK):
        start = chunk * CHUNK
        for block in range(D // 256):
            cut = vectors[start : start + CHUNK, block * 256 : (block + 1) * 256]
            spread_own[block * 256 : (block + 1) * 256, start : start + CHUNK] = nt(
                eye256, cut
            ).astype(BF16)
        lay_codes(first[start : start + CHUNK, :] + 1, high_own, low_own, 0, start)
        lay_codes(second[start : start + CHUNK, :] + 1, high_own, low_own, 1, start)

    def own_step(turn, unused):
        for side in range(2):
            owner = spot_of(turn) * 2 + side
            for index in range(2):
                sums, count = tally(
                    spread_own,
                    owner * 32,
                    high_own,
                    low_own,
                    owner,
                    range(ROWS_DEV // WIDE),
                    index,
                    True,
                )
                for value in range(8):
                    z_of, at = value // 2, 2 * index + value % 2
                    parts[side, turn, z_of, at] = sums[value]
                    counts[side, turn, z_of, at : at + 1, :] = count[value : value + 1]
        return unused


    lax.fori_loop(0, 16, own_step, 0)

    mate_id = (rows_at + 1 - 2 * core, z)
    count_swap = pltpu.make_async_remote_copy(
        src_ref=counts.at[1 - core],
        dst_ref=count_mate,
        send_sem=swap_send,
        recv_sem=swap_recv,
        device_id=mate_id,
        device_id_type=MESH,
    )
    count_swap.start()

    def count_copy(turn, z_step):
        z_to = lax.rem(z + z_step, 4)
        return pltpu.make_async_remote_copy(
            src_ref=count_half.at[turn, z_to],
            dst_ref=count_landed.at[turn * 4 + 3 - z_step],
            send_sem=count_send,
            recv_sem=count_recv,
            device_id=(spot_of(turn) * 2 + core, z_to),
            device_id_type=MESH,
        )

    def send_counts(step, unused):
        turn = step // 4
        count_copy(turn, 3 - lax.rem(step, 4)).start()
        return unused

    loads[4].wait()
    ones128 = jnp.ones((128, 128), BF16)

    def lay_asked(chunk):
        arrived = recv.at[pl.ds(max(32 * chunk, 1), 32 if chunk else 31)]
        pltpu.make_async_copy(arrived, arrived, recv_sem.at[chunk]).wait()
        start = chunk * CHUNK
        codes = recv[32 * chunk : 32 * chunk + 32, 0:8, :].reshape(CHUNK, 128)
        lay_codes(codes & 65535, high_asked, low_asked, 0, start)
        lay_codes(codes >> 16, high_asked, low_asked, 1, start)
        slots_in = recv[32 * chunk : 32 * chunk + 32, 8:9, :].reshape(32, 128)
        row_at = iota((CHUNK, 128), 0)
        lane = iota((CHUNK, 128), 1)
        fan = one_hot((iota((CHUNK, 32), 0) >> 3) == iota((CHUNK, 32), 1))
        keep = (row_at & 7) == lane
        slot_high = nn(fan, narrow(slots_in >> 7))
        slot_low = nn(fan, narrow(slots_in & 127))
        slot_high = nn(jnp.where(keep, slot_high, 0.0).astype(BF16), ones128).astype(BF16)
        slot_low = nn(jnp.where(keep, slot_low, 0.0).astype(BF16), ones128).astype(BF16)
        low_hot = jnp.where(slot_low == narrow(lane), one, zero)
        for block in range(CENT_DEV // 128):
            wanted[start : start + CHUNK, block * 128 : (block + 1) * 128] = jnp.where(
                slot_high == jnp.full((), block, BF16), low_hot, zero
            )

    def fetch(block, low_chunk, high_chunk):
        x_to = lax.rem(x + block + 1, 4)
        columns = pl.ds(pl.multiple_of(x_to * 256, 256), 256)
        base = nn(
            wanted[low_chunk * CHUNK : high_chunk * CHUNK, :], table[:, columns]
        ).astype(BF16)
        for chunk in range(low_chunk, high_chunk):
            at = (chunk - low_chunk) * CHUNK
            spread_asked[:, chunk * CHUNK : (chunk + 1) * CHUNK] = nt(
                -eye256, base[at : at + CHUNK]
            ).astype(BF16)

    def add_asked(turn, side, low_chunk, high_chunk):
        spot = spot_of(turn)
        for index in range(2):
            sums, unused_count = tally(
                spread_asked,
                (lax.rem(spot, 4) * 2 + side) * 32,
                high_asked,
                low_asked,
                spot * 2 + side,
                range(low_chunk * CHUNK // WIDE, high_chunk * CHUNK // WIDE),
                index,
                False,
            )
            for value in range(8):
                parts[side, turn, value // 2, 2 * index + value % 2] += sums[value]

    def early_block(block, unused):
        fetch(block, 0, 1)

        def early_step(step, unused_too):
            for side in range(2):
                add_asked(block * 4 + step, side, 0, 1)
            return unused_too

        lax.fori_loop(0, 4, early_step, 0)
        return unused

    for chunk in range(ASKED // CHUNK):
        lay_asked(chunk)

    def core_copy(turn):
        return pltpu.make_async_remote_copy(
            src_ref=parts.at[1 - core, turn],
            dst_ref=mate.at[turn],
            send_sem=core_send.at[turn],
            recv_sem=core_recv.at[turn],
            device_id=mate_id,
            device_id_type=MESH,
        )

    def part_copy(turn, z_step):
        z_to = lax.rem(z + z_step, 4)
        return pltpu.make_async_remote_copy(
            src_ref=half.at[turn, z_to],
            dst_ref=landed.at[turn * 4 + 3 - z_step],
            send_sem=part_send,
            recv_sem=part_recv.at[turn // SPLIT],
            device_id=(spot_of(turn) * 2 + core, z_to),
            device_id_type=MESH,
        )

    def pass_on(turn):
        core_copy(turn).wait_recv()
        half[turn] = parts[core, turn] + mate[turn]
        for z_step in range(1, 4):
            part_copy(turn, z_step).start()

        @pl.when(turn != 15)
        def _():
            part_copy(turn, 0).start()

    def block_step(block, unused):
        fetch(block, 0, ASKED // CHUNK)

        @pl.when(block == 1)
        def _():
            count_swap.wait_recv()
            count_half[...] = counts[core] + count_mate[...]
            lax.fori_loop(0, 63, send_counts, 0)


        def spot_step(spot, unused_too):
            turn = block * 4 + spot

            for side in range(2):
                add_asked(turn, side, 0, ASKED // CHUNK)
            core_copy(turn).start()

            @pl.when(turn >= LAG)
            def _():
                pass_on(turn - LAG)

            return unused_too

        lax.fori_loop(0, 4, spot_step, 0)
        return unused

    lax.fori_loop(0, 4, block_step, 0)
    for turn in range(16 - LAG, 16):
        pass_on(jnp.int32(turn))

    pltpu.make_async_copy(count_landed, count_landed, count_recv).wait()
    count = count_half[15, z]
    for step in range(63):
        count = count + count_landed[step]
    count = jnp.maximum(count, 1.0)

    total = half[15, z]
    for group, (begin, end) in enumerate(((0, 4 * SPLIT), (4 * SPLIT, 63))):
        others = landed.at[pl.ds(begin, end - begin)]
        pltpu.make_async_copy(others, others, part_recv.at[group]).wait()
        for step in range(begin, end):
            total = total + landed[step]

    for at in range(4):
        means[z, at] = total[at] / count[at : at + 1, :]

    for z_step in range(1, 4):
        pltpu.make_async_remote_copy(
            src_ref=means.at[z],
            dst_ref=means.at[z],
            send_sem=last_send,
            recv_sem=last_recv,
            device_id=(rows_at, lax.rem(z + z_step, 4)),
            device_id_type=MESH,
        ).start()
    all_landed = landed.at[pl.ds(0, 63)]
    pltpu.make_async_copy(all_landed, all_landed, part_send).wait()
    pltpu.make_async_copy(count_landed, count_landed, count_send).wait()
    count_swap.wait_send()
    rest = send.at[pl.ds(1, DEV - 1)]
    pltpu.make_async_copy(rest, rest, send_sem).wait()

    def end_core(turn, unused):
        core_copy(turn).wait_send()
        return unused

    lax.fori_loop(0, 16, end_core, 0)
    three = means.at[pl.ds(0, 3)]
    pltpu.make_async_copy(three, three, last_send).wait()
    pltpu.make_async_copy(three, three, last_recv).wait()
    for index, out in ((0, out_first), (1, out_second)):
        for sub in range(4):
            out[8 * sub : 8 * sub + 8, :] = jnp.concatenate(
                [
                    means[v // 2, 2 * index + v % 2][:, 32 * sub : 32 * sub + 32]
                    for v in range(8)
                ],
                axis=1,
            )


def hand_on(first, second, out_first, out_second):
    out_first[...] = first[...]
    out_second[...] = second[...]


def on_device(vectors, list_ids, centroids, list_place, codes_first, codes_second):
    place = list_place.reshape(2048, 128)
    vmem, dma = pltpu.VMEM, pltpu.SemaphoreType.DMA
    first, second = pl.pallas_call(
        kernel,
        out_shape=[jax.ShapeDtypeStruct((32, K), F32)] * 2,
        in_specs=[pl.BlockSpec(memory_space=pl.ANY)] * 6,
        out_specs=[pl.BlockSpec(memory_space=pltpu.VMEM)] * 2,
        scratch_shapes=[
            pltpu.SMEM((ROWS_DEV,), I32),
            vmem((2048, 128), I32),
            vmem((ROWS_DEV, S), I32),
            vmem((ROWS_DEV, S), I32),
            vmem((ROWS_DEV, D), BF16),
            vmem((CENT_DEV, D), BF16),
            vmem((ROWS_DEV, 128), I32),
            vmem((ROWS_DEV, ROWS_DEV), BF16),
            vmem((DEV, 9, 128), I32),
            vmem((DEV, 9, 128), I32),
            vmem((D, ROWS_DEV), BF16),
            vmem((2, S, ROWS_DEV), F32),
            vmem((2, S, ROWS_DEV), F32),
            vmem((ASKED, CENT_DEV), BF16),
            vmem((256, ASKED), BF16),
            vmem((2, S, ASKED), F32),
            vmem((2, S, ASKED), F32),
            vmem((2, 16, 4, 4, 8, 128), F32),
            vmem((16, 4, 4, 8, 128), F32),
            vmem((16, 4, 4, 8, 128), F32),
            vmem((63, 4, 8, 128), F32),
            vmem((2, 16, 4, 4, 128), F32),
            vmem((16, 4, 4, 128), F32),
            vmem((16, 4, 4, 128), F32),
            vmem((63, 4, 128), F32),
            vmem((4, 4, 8, 128), F32),
            dma((6,)),
            dma,
            dma((4,)),
            dma((16,)),
            dma((16,)),
            dma,
            dma((2,)),
            dma,
            dma,
            dma,
            dma,
            dma,
            dma,
        ],
        compiler_params=pltpu.CompilerParams(
            collective_id=0, has_side_effects=True, vmem_limit_bytes=55130 * 1024
        ),
        name="codebooks",
    )(list_ids, place, codes_first, codes_second, vectors, centroids)
    first, second = pl.pallas_call(
        hand_on,
        out_shape=[jax.ShapeDtypeStruct((32, K), F32)] * 2,
        in_specs=[pl.BlockSpec(memory_space=vmem)] * 2,
        out_specs=[pl.BlockSpec(memory_space=vmem)] * 2,
        compiler_params=pltpu.CompilerParams(vmem_limit_bytes=2**20),
        name="hand_on",
    )(first, second)
    return (first.T, second.T)


def solution(mesh):
    return jax.shard_map(
        on_device,
        mesh=mesh,
        in_specs=(
            P(("rows", "rep"), None),
            P(("rows", "rep")),
            P(("rows", "rep"), None),
            P(),
            P(("rows", "rep"), None),
            P(("rows", "rep"), None),
        ),
        out_specs=(P(None, "rows"), P(None, "rows")),
        check_vma=False,
    )
```

```python
import jax
import jax.numpy as jnp
from jax import lax
from jax.experimental import pallas as pl
from jax.experimental.pallas import tpu as pltpu
from jax.sharding import PartitionSpec as P

K = 256
D = 1024
S = 128
DEV = 128
CAP = 8
ROWS_DEV = 512
CENT_DEV = 2048
ASKED = DEV * CAP
CHUNK = 256
WIDE = 512
LAG = 2
SPLIT = 12
MESH = pl.DeviceIdType.MESH
F32 = jnp.float32
BF16 = jnp.bfloat16
I32 = jnp.int32


def iota(shape, dim):
    return lax.broadcasted_iota(I32, shape, dim)


def nt(a, b):
    return lax.dot_general(a, b, (((1,), (1,)), ((), ())), preferred_element_type=F32)


def nn(a, b):
    return jnp.dot(a, b, preferred_element_type=F32)


def one_hot(match):
    return jnp.where(match, 1.0, 0.0).astype(BF16)


def narrow(whole):
    return whole.astype(F32).astype(BF16)


def kernel(
    ids_hbm,
    place_hbm,
    first_hbm,
    second_hbm,
    vectors_hbm,
    table_hbm,
    out_first,
    out_second,
    ids,
    place,
    first,
    second,
    vectors,
    table,
    found,
    earlier,
    send,
    recv,
    spread_own,
    high_own,
    low_own,
    wanted,
    spread_asked,
    high_asked,
    low_asked,
    parts,
    mate,
    half,
    landed,
    counts,
    count_mate,
    count_half,
    count_landed,
    means,
    load_sem,
    send_sem,
    recv_sem,
    core_send,
    core_recv,
    part_send,
    part_recv,
    swap_send,
    swap_recv,
    count_send,
    count_recv,
    last_send,
    last_recv,
):
    rows_at = lax.axis_index("rows")
    z = lax.axis_index("rep")
    me = rows_at * 4 + z
    core = lax.rem(rows_at, 2)
    y = lax.rem(rows_at // 2, 4)
    x = rows_at // 8
    barrier = pltpu.get_barrier_semaphore()

    loads = []
    for at, (source, target) in enumerate(
        (
            (place_hbm, place),
            (first_hbm, first),
            (second_hbm, second),
            (vectors_hbm, vectors),
            (table_hbm, table),
            (ids_hbm, ids),
        )
    ):
        load = pltpu.make_async_copy(source, target, load_sem.at[at])
        loads.append(load)
    for at in (5, 0, 1, 2):
        loads[at].start()

    def greet(step, unused):
        other = (me + step) & (DEV - 1)
        pl.semaphore_signal(
            barrier, inc=1, device_id=(other >> 2, other & 3), device_id_type=MESH
        )
        return unused

    lax.fori_loop(1, DEV, greet, 0)

    earlier[...] = one_hot(iota((ROWS_DEV, ROWS_DEV), 0) < iota((ROWS_DEV, ROWS_DEV), 1))

    loads[5].wait()
    loads[0].wait()
    loads[3].start()
    loads[4].start()
    lanes = iota((1, 128), 1)

    def find(block, unused):
        for step in range(8):
            row = block * 8 + step
            wish = ids[row]
            found[pl.ds(row, 1), :] = jnp.where(
                lanes == (wish & 127), place[pl.ds(wish >> 7, 1), :], 0
            )
        return unused

    lax.fori_loop(0, ROWS_DEV // 8, find, 0)

    places = found[...]
    ones8 = jnp.ones((8, 128), BF16)
    owner_row = nt(ones8, narrow(places >> 11))[0:1, :].astype(I32)
    slot_high = nt(ones8, narrow((places >> 7) & 15))[0:1, :]
    slot_low = nt(ones8, narrow(places & 127))[0:1, :]
    owner_is = iota((DEV, ROWS_DEV), 0) == owner_row
    owner_hot = one_hot(owner_is)
    before = nn(owner_hot, earlier[...])
    rank = jnp.sum(jnp.where(owner_is, before, 0.0), axis=0, keepdims=True).astype(I32)
    rank_is = iota((DEV, ROWS_DEV), 0) == rank
    slots_high = nt(owner_hot, jnp.where(rank_is, slot_high, 0.0).astype(BF16))
    slots_low = nt(owner_hot, jnp.where(rank_is, slot_low, 0.0).astype(BF16))
    slots = (slots_high * 128.0 + slots_low).astype(I32)
    position = owner_row * CAP + rank
    loads[1].wait()
    loads[2].wait()
    payload = jnp.concatenate([narrow(first[...] + 1), narrow(second[...] + 1)], axis=1)
    for block in range(4):
        move = one_hot(iota((256, ROWS_DEV), 0) + 256 * block == position)
        moved = nn(move, payload).astype(I32)
        codes = moved[:, 0:128] + moved[:, 128:256] * 65536
        send[32 * block : 32 * block + 32, 0:8, :] = codes.reshape(32, CAP, 128)
    send[:, 8:9, :] = slots.reshape(DEV, 1, 128)

    pl.semaphore_wait(barrier, DEV - 1)

    def push(step, unused):
        other = (me + step) & (DEV - 1)
        pltpu.make_async_remote_copy(
            src_ref=send.at[other],
            dst_ref=recv.at[step],
            send_sem=send_sem,
            recv_sem=recv_sem.at[step >> 5],
            device_id=(other >> 2, other & 3),
            device_id_type=MESH,
        ).start()
        return unused

    lax.fori_loop(1, DEV, push, 0)
    recv[0] = send[me]

    def lay_codes(column, high, low, index, start):
        turned = nt(eye128, narrow(column)) - 1.0
        low_part = jnp.floor(turned * (1.0 / 32.0))
        high_part = turned - 32.0 * low_part
        high[index, :, start : start + CHUNK] = high_part
        low[index, :, start : start + CHUNK] = low_part

    eye128 = one_hot(iota((128, 128), 0) == iota((128, 128), 1))
    eye256 = one_hot(iota((256, 256), 0) == iota((256, 256), 1))

    high_is = narrow(iota((16, WIDE), 0))
    lane_sub = iota((8, 128), 1) >> 5
    count_is = narrow(iota((16, WIDE), 0) & 7)
    one = jnp.ones((), BF16)
    zero = jnp.zeros((), BF16)

    def tally(spread, row, high, low, owner, chunks, index, counting):
        total = None
        for chunk in chunks:
            start = chunk * WIDE
            left, right, mark = [], [], []
            for pair in range(2):
                data = spread[
                    pl.ds(pl.multiple_of(row + 16 * pair, 16), 16), start : start + WIDE
                ]
                lows = []
                for sub in range(2):
                    at = owner * 4 + pair * 2 + sub
                    h = jnp.broadcast_to(high[index, pl.ds(at, 1), start : start + WIDE], (8, WIDE))
                    h = jnp.concatenate([h, h], axis=0).astype(BF16)
                    left.append(jnp.where(h == high_is, one, zero))
                    left.append(jnp.where(h == high_is + 16.0, one, zero))
                    lows.append(
                        jnp.broadcast_to(low[index, pl.ds(at, 1), start : start + WIDE], (8, WIDE))
                    )
                l = jnp.concatenate(lows, axis=0).astype(BF16)
                for value in range(8):
                    right.append(jnp.where(l == jnp.full((), value, BF16), data, zero))
                if counting:
                    mark.append(jnp.where(l == count_is, one, zero))
            product = nt(jnp.concatenate(right + mark, axis=0), jnp.concatenate(left, axis=0))
            total = product if total is None else total + product

        def own_lanes(rows):
            mine = total[rows[0] : rows[0] + 8]
            for sub in range(1, 4):
                mine = jnp.where(lane_sub == sub, total[rows[sub] : rows[sub] + 8], mine)
            return mine

        sums = [own_lanes([16 * v, 16 * v + 8, 128 + 16 * v, 136 + 16 * v]) for v in range(8)]
        return sums, own_lanes([256, 264, 272, 280]) if counting else None

    def spot_of(turn):
        x_to = (x + (turn >> 2) + 1) & 3
        y_to = (y + turn + 1) & 3
        return x_to * 4 + y_to

    loads[3].wait()
    for chunk in range(ROWS_DEV // CHUNK):
        start = chunk * CHUNK
        for block in range(D // 256):
            cut = vectors[start : start + CHUNK, block * 256 : (block + 1) * 256]
            spread_own[block * 256 : (block + 1) * 256, start : start + CHUNK] = nt(
                eye256, cut
            ).astype(BF16)
        lay_codes(first[start : start + CHUNK, :] + 1, high_own, low_own, 0, start)
        lay_codes(second[start : start + CHUNK, :] + 1, high_own, low_own, 1, start)

    def own_step(turn, unused):
        for side in range(2):
            owner = spot_of(turn) * 2 + side
            for index in range(2):
                sums, count = tally(
                    spread_own,
                    owner * 32,
                    high_own,
                    low_own,
                    owner,
                    range(ROWS_DEV // WIDE),
                    index,
                    True,
                )
                for value in range(8):
                    z_of, at = value // 2, 2 * index + value % 2
                    parts[side, turn, z_of, at] = sums[value]
                    counts[side, turn, z_of, at : at + 1, :] = count[value : value + 1]
        return unused


    lax.fori_loop(0, 16, own_step, 0)

    mate_id = (rows_at + 1 - 2 * core, z)
    count_swap = pltpu.make_async_remote_copy(
        src_ref=counts.at[1 - core],
        dst_ref=count_mate,
        send_sem=swap_send,
        recv_sem=swap_recv,
        device_id=mate_id,
        device_id_type=MESH,
    )
    count_swap.start()

    def count_copy(turn, z_step):
        z_to = (z + z_step) & 3
        return pltpu.make_async_remote_copy(
            src_ref=count_half.at[turn, z_to],
            dst_ref=count_landed.at[turn * 4 + 3 - z_step],
            send_sem=count_send,
            recv_sem=count_recv,
            device_id=(spot_of(turn) * 2 + core, z_to),
            device_id_type=MESH,
        )

    def send_counts(step, unused):
        turn = step >> 2
        count_copy(turn, 3 - (step & 3)).start()
        return unused

    loads[4].wait()
    ones128 = jnp.ones((128, 128), BF16)

    def lay_asked(chunk):
        arrived = recv.at[pl.ds(max(32 * chunk, 1), 32 if chunk else 31)]
        pltpu.make_async_copy(arrived, arrived, recv_sem.at[chunk]).wait()
        start = chunk * CHUNK
        codes = recv[32 * chunk : 32 * chunk + 32, 0:8, :].reshape(CHUNK, 128)
        lay_codes(codes & 65535, high_asked, low_asked, 0, start)
        lay_codes(codes >> 16, high_asked, low_asked, 1, start)
        slots_in = recv[32 * chunk : 32 * chunk + 32, 8:9, :].reshape(32, 128)
        row_at = iota((CHUNK, 128), 0)
        lane = iota((CHUNK, 128), 1)
        fan = one_hot((iota((CHUNK, 32), 0) >> 3) == iota((CHUNK, 32), 1))
        keep = (row_at & 7) == lane
        slot_high = nn(fan, narrow(slots_in >> 7))
        slot_low = nn(fan, narrow(slots_in & 127))
        slot_high = nn(jnp.where(keep, slot_high, 0.0).astype(BF16), ones128).astype(BF16)
        slot_low = nn(jnp.where(keep, slot_low, 0.0).astype(BF16), ones128).astype(BF16)
        low_hot = jnp.where(slot_low == narrow(lane), one, zero)
        for block in range(CENT_DEV // 128):
            wanted[start : start + CHUNK, block * 128 : (block + 1) * 128] = jnp.where(
                slot_high == jnp.full((), block, BF16), low_hot, zero
            )

    def fetch(block, low_chunk, high_chunk):
        x_to = lax.rem(x + block + 1, 4)
        columns = pl.ds(pl.multiple_of(x_to * 256, 256), 256)
        base = nn(
            wanted[low_chunk * CHUNK : high_chunk * CHUNK, :], table[:, columns]
        ).astype(BF16)
        for chunk in range(low_chunk, high_chunk):
            at = (chunk - low_chunk) * CHUNK
            spread_asked[:, chunk * CHUNK : (chunk + 1) * CHUNK] = nt(
                -eye256, base[at : at + CHUNK]
            ).astype(BF16)

    def add_asked(turn, side, low_chunk, high_chunk):
        spot = spot_of(turn)
        for index in range(2):
            sums, unused_count = tally(
                spread_asked,
                ((spot & 3) * 2 + side) * 32,
                high_asked,
                low_asked,
                spot * 2 + side,
                range(low_chunk * CHUNK // WIDE, high_chunk * CHUNK // WIDE),
                index,
                False,
            )
            for value in range(8):
                parts[side, turn, value // 2, 2 * index + value % 2] += sums[value]

    def early_block(block, unused):
        fetch(block, 0, 1)

        def early_step(step, unused_too):
            for side in range(2):
                add_asked(block * 4 + step, side, 0, 1)
            return unused_too

        lax.fori_loop(0, 4, early_step, 0)
        return unused

    for chunk in range(ASKED // CHUNK):
        lay_asked(chunk)

    def core_copy(turn):
        return pltpu.make_async_remote_copy(
            src_ref=parts.at[1 - core, turn],
            dst_ref=mate.at[turn],
            send_sem=core_send.at[turn],
            recv_sem=core_recv.at[turn],
            device_id=mate_id,
            device_id_type=MESH,
        )

    def part_copy(turn, z_step):
        z_to = (z + z_step) & 3
        return pltpu.make_async_remote_copy(
            src_ref=half.at[turn, z_to],
            dst_ref=landed.at[turn * 4 + 3 - z_step],
            send_sem=part_send,
            recv_sem=part_recv.at[jnp.where(turn < SPLIT, 0, 1)],
            device_id=(spot_of(turn) * 2 + core, z_to),
            device_id_type=MESH,
        )

    def pass_on(turn):
        core_copy(turn).wait_recv()
        half[turn] = parts[core, turn] + mate[turn]
        for z_step in range(1, 4):
            part_copy(turn, z_step).start()

        @pl.when(turn != 15)
        def _():
            part_copy(turn, 0).start()

    def block_step(block, unused):
        fetch(block, 0, ASKED // CHUNK)

        @pl.when(block == 1)
        def _():
            count_swap.wait_recv()
            count_half[...] = counts[core] + count_mate[...]
            lax.fori_loop(0, 63, send_counts, 0)


        def spot_step(spot, unused_too):
            turn = block * 4 + spot

            for side in range(2):
                add_asked(turn, side, 0, ASKED // CHUNK)
            core_copy(turn).start()

            @pl.when(turn >= LAG)
            def _():
                pass_on(turn - LAG)

            return unused_too

        lax.fori_loop(0, 4, spot_step, 0)
        return unused

    lax.fori_loop(0, 4, block_step, 0)
    for turn in range(16 - LAG, 16):
        pass_on(jnp.int32(turn))

    pltpu.make_async_copy(count_landed, count_landed, count_recv).wait()
    count = count_half[15, z]
    for step in range(63):
        count = count + count_landed[step]
    count = jnp.maximum(count, 1.0)

    total = half[15, z]
    for group, (begin, end) in enumerate(((0, 4 * SPLIT), (4 * SPLIT, 63))):
        others = landed.at[pl.ds(begin, end - begin)]
        pltpu.make_async_copy(others, others, part_recv.at[group]).wait()
        for step in range(begin, end):
            total = total + landed[step]

    for at in range(4):
        means[z, at] = total[at] / count[at : at + 1, :]

    for z_step in range(1, 4):
        pltpu.make_async_remote_copy(
            src_ref=means.at[z],
            dst_ref=means.at[z],
            send_sem=last_send,
            recv_sem=last_recv,
            device_id=(rows_at, lax.rem(z + z_step, 4)),
            device_id_type=MESH,
        ).start()
    all_landed = landed.at[pl.ds(0, 63)]
    pltpu.make_async_copy(all_landed, all_landed, part_send).wait()
    pltpu.make_async_copy(count_landed, count_landed, count_send).wait()
    count_swap.wait_send()
    rest = send.at[pl.ds(1, DEV - 1)]
    pltpu.make_async_copy(rest, rest, send_sem).wait()

    def end_core(turn, unused):
        core_copy(turn).wait_send()
        return unused

    lax.fori_loop(0, 16, end_core, 0)
    three = means.at[pl.ds(0, 3)]
    pltpu.make_async_copy(three, three, last_send).wait()
    pltpu.make_async_copy(three, three, last_recv).wait()
    for index, out in ((0, out_first), (1, out_second)):
        for sub in range(4):
            out[8 * sub : 8 * sub + 8, :] = jnp.concatenate(
                [
                    means[v // 2, 2 * index + v % 2][:, 32 * sub : 32 * sub + 32]
                    for v in range(8)
                ],
                axis=1,
            )


def hand_on(first, second, out_first, out_second):
    out_first[...] = first[...]
    out_second[...] = second[...]


def on_device(vectors, list_ids, centroids, list_place, codes_first, codes_second):
    place = list_place.reshape(2048, 128)
    vmem, dma = pltpu.VMEM, pltpu.SemaphoreType.DMA
    first, second = pl.pallas_call(
        kernel,
        out_shape=[jax.ShapeDtypeStruct((32, K), F32)] * 2,
        in_specs=[pl.BlockSpec(memory_space=pl.ANY)] * 6,
        out_specs=[pl.BlockSpec(memory_space=pltpu.VMEM)] * 2,
        scratch_shapes=[
            pltpu.SMEM((ROWS_DEV,), I32),
            vmem((2048, 128), I32),
            vmem((ROWS_DEV, S), I32),
            vmem((ROWS_DEV, S), I32),
            vmem((ROWS_DEV, D), BF16),
            vmem((CENT_DEV, D), BF16),
            vmem((ROWS_DEV, 128), I32),
            vmem((ROWS_DEV, ROWS_DEV), BF16),
            vmem((DEV, 9, 128), I32),
            vmem((DEV, 9, 128), I32),
            vmem((D, ROWS_DEV), BF16),
            vmem((2, S, ROWS_DEV), F32),
            vmem((2, S, ROWS_DEV), F32),
            vmem((ASKED, CENT_DEV), BF16),
            vmem((256, ASKED), BF16),
            vmem((2, S, ASKED), F32),
            vmem((2, S, ASKED), F32),
            vmem((2, 16, 4, 4, 8, 128), F32),
            vmem((16, 4, 4, 8, 128), F32),
            vmem((16, 4, 4, 8, 128), F32),
            vmem((63, 4, 8, 128), F32),
            vmem((2, 16, 4, 4, 128), F32),
            vmem((16, 4, 4, 128), F32),
            vmem((16, 4, 4, 128), F32),
            vmem((63, 4, 128), F32),
            vmem((4, 4, 8, 128), F32),
            dma((6,)),
            dma,
            dma((4,)),
            dma((16,)),
            dma((16,)),
            dma,
            dma((2,)),
            dma,
            dma,
            dma,
            dma,
            dma,
            dma,
        ],
        compiler_params=pltpu.CompilerParams(
            collective_id=0, has_side_effects=True, vmem_limit_bytes=55130 * 1024
        ),
        name="codebooks",
    )(list_ids, place, codes_first, codes_second, vectors, centroids)
    first, second = pl.pallas_call(
        hand_on,
        out_shape=[jax.ShapeDtypeStruct((32, K), F32)] * 2,
        in_specs=[pl.BlockSpec(memory_space=vmem)] * 2,
        out_specs=[pl.BlockSpec(memory_space=vmem)] * 2,
        compiler_params=pltpu.CompilerParams(vmem_limit_bytes=2**20),
        name="hand_on",
    )(first, second)
    return (first.T, second.T)


def solution(mesh):
    return jax.shard_map(
        on_device,
        mesh=mesh,
        in_specs=(
            P(("rows", "rep"), None),
            P(("rows", "rep")),
            P(("rows", "rep"), None),
            P(),
            P(("rows", "rep"), None),
            P(("rows", "rep"), None),
        ),
        out_specs=(P(None, "rows"), P(None, "rows")),
        check_vma=False,
    )
```
